256 devices in a mesh: cells: 64 (over y_lo, x, z), tracers: 4 (over y_hi, core).
Axes of the slice: x: 4, y: 4 (y_hi: 2, y_lo: 2; y = y_hi * 2 + y_lo), z: 8, core: 2. Of those that a mesh axis runs over, the one named last changes fastest.
Arguments:
- tracers: float32 [256, 6, 384, 128], P('tracers', None, 'cells'), may hold values from 0 to 18, as said below
- hour_fields: float32 [4, 10, 6, 384, 128], P('tracers', None, None, 'cells'), may hold values from -1 to 2, as said below
- reader_table: int32 [64], P('cells'), may hold values from 0 to 3
Outputs:
- transported: float32 [256, 6, 384, 128], P('tracers', None, 'cells')
The draws below stay inside these ranges and needn't reach their ends.
Inputs may be any that keep to these rules, and one draw needn't show every extreme that they name: `reader_table`: tracers index of the device whose copy of hour_fields is valid for this block. `tracers`: positive mixing ratios. `hour_fields`: rows 0 and 1 are Courant numbers of magnitude below 1, rows 2 and 3 positive pressure thicknesses, rows from 4 on the given inverse of each column's implicit diffusion matrix.
All inputs are finite; a program needn't handle non-finite values.
Results may differ from the reference program's by a relative error of at most 0.0003.
Values sent between devices are 32-bit elements; how exact they have to be, the bound alone decides.
No kernel may reach another device: no remote copies, remote signals or barrier semaphores. Data moves between devices by JAX's collectives and lax.ppermute only.
A program may use at most 64 MiB of HBM per device.

```python
import jax
import jax.numpy as jnp
from jax import lax

NTR = 256
LEV = 6
CX = 6
READERS = 4
BLOCKS = 64
NX = 384
NY = 128


def draw_tracers(key, part):
    key = jax.random.fold_in(key, 11)
    xs = jnp.arange(NX, dtype=jnp.float32) / max(NX - 1, 1)
    ys = jnp.arange(NY, dtype=jnp.float32) / max(NY - 1, 1)
    values = jax.random.uniform(key, (NTR, LEV, NX, NY), jnp.float32, 0.5, 1.5)
    exponent = 0.5 * (xs[:, None] + ys[None, :]) - 0.5
    return values * jnp.power(10.0, exponent)


def draw_hour_fields(key, part):
    key = jax.random.fold_in(key, 23)
    keys = jax.random.split(key, 6)
    shape = (READERS, 1, LEV, NX, NY)
    reach = 0.9
    spread = 0.0
    courant_x = jax.random.uniform(keys[0], shape, jnp.float32, -reach, reach)
    courant_y = jax.random.uniform(keys[1], shape, jnp.float32, -reach, reach)
    dp_old = jax.random.uniform(keys[2], shape, jnp.float32, 0.5, 1.5)
    dp_new = jax.random.uniform(keys[3], shape, jnp.float32, 0.6, 2.0)
    levels = jnp.arange(LEV, dtype=jnp.float32)
    distance = jnp.abs(levels[:, None] - levels[None, :])[None, :, :, None, None]
    off_diag = jax.random.uniform(keys[4], (READERS, LEV, LEV, NX, NY), jnp.float32, spread, 1.0) * 0.6 / (1.0 + distance)
    diagonal = jax.random.uniform(keys[5], (READERS, LEV, LEV, NX, NY), jnp.float32, 0.4, 0.8)
    inverse = jnp.where(distance == 0.0, diagonal, off_diag)
    return jnp.concatenate([courant_x, courant_y, dp_old, dp_new, inverse], axis=1)


def set_ends(entries, rng, smallest, top_value):
    longest = entries.shape.index(max(entries.shape))
    spots = []
    for shift in (0, 1):
        where = [jax.random.randint(jax.random.fold_in(rng, axis), (), 0, length) for axis, length in enumerate(entries.shape)]
        where[longest] = (where[longest] + shift) % entries.shape[longest]
        spots.append(tuple(where))
    return entries.at[spots[0]].set(smallest).at[spots[1]].set(top_value)


def setup_inputs(seed: int = 0) -> dict:
    splits = jax.random.split(jax.random.key(seed), 4)
    return {
        "tracers": draw_tracers(jax.random.fold_in(splits[3], 71), 0),
        "hour_fields": draw_hour_fields(jax.random.fold_in(splits[3], 71), 0),
        "reader_table": set_ends(jax.random.randint(splits[2], (BLOCKS,), 0, READERS), jax.random.fold_in(splits[2], 1), 0, READERS - 1).astype(jnp.int32),
    }


def window(array, start, count, along):
    return lax.slice_in_dim(array, start, start + count, axis=array.ndim + along)


def ppm_sweep(extended, courant, along):
    inner = extended.shape[extended.ndim + along] - 6
    edge_val = (7.0 / 12.0) * (window(extended, 1, inner + 3, along) + window(extended, 2, inner + 3, along)) - (1.0 / 12.0) * (window(extended, 0, inner + 3, along) + window(extended, 3, inner + 3, along))
    left_edge = window(edge_val, 0, inner + 2, along)
    right_edge = window(edge_val, 1, inner + 2, along)
    centre = window(extended, 2, inner + 2, along)
    slope_part = right_edge - left_edge
    curvature = 6.0 * (centre - 0.5 * (left_edge + right_edge))
    upwind_pos = window(right_edge, 0, inner + 1, along) - 0.5 * courant * (window(slope_part, 0, inner + 1, along) - (1.0 - (2.0 / 3.0) * courant) * window(curvature, 0, inner + 1, along))
    backward = -courant
    upwind_neg = window(left_edge, 1, inner + 1, along) + 0.5 * backward * (window(slope_part, 1, inner + 1, along) + (1.0 - (2.0 / 3.0) * backward) * window(curvature, 1, inner + 1, along))
    fluxes = courant * jnp.where(courant >= 0, upwind_pos, upwind_neg)
    return window(extended, 3, inner, along) - (window(fluxes, 1, inner, along) - window(fluxes, 0, inner, along))


def sweep_walls(field, courant_y):
    extended = jnp.concatenate([field[..., :1]] * 3 + [field] + [field[..., -1:]] * 3, axis=-1)
    zero_face = jnp.zeros_like(courant_y[..., :1])
    faces = jnp.concatenate([zero_face, courant_y[..., 1:], zero_face], axis=-1)
    return ppm_sweep(extended, faces, -1)


def sweep_periodic(field, courant_x):
    extended = jnp.concatenate([field[:, -3:], field, field[:, :3]], axis=1)
    faces = jnp.concatenate([courant_x, courant_x[:, :1]], axis=1)
    return ppm_sweep(extended, 0.5 * faces, -2)


def reference(tracers, hour_fields, reader_table):
    owner = jnp.repeat(reader_table, CX)
    select = (owner[None, :] == jnp.arange(READERS, dtype=jnp.int32)[:, None]).astype(jnp.float32)
    fields = jnp.sum(select[:, None, None, :, None] * hour_fields, axis=0)
    courant_x = fields[0]
    courant_y = fields[1]
    dp_old = fields[2]
    dp_new = fields[3]
    inverse = fields[4:]

    def advance(field):
        first = sweep_periodic(field, courant_x)
        second = sweep_walls(first, courant_y)
        third = sweep_periodic(second, courant_x)
        diffused = jnp.einsum("lmxy,mxy->lxy", inverse, third, precision=lax.Precision.HIGHEST)
        before = jnp.sum(field * dp_old)
        after = jnp.sum(diffused * dp_new)
        return diffused * (before / after)

    return lax.map(advance, tracers)
```

```python
import functools

import jax
import jax.numpy as jnp
from jax import lax
from jax.experimental import pallas as pl
from jax.experimental.pallas import tpu as pltpu
from jax.sharding import PartitionSpec as P

LEV, CX, NY = 6, 6, 128
ROWS = LEV * CX
NF = 10
HALO = 3
WIDE = CX + 2 * HALO
F32 = jnp.float32
VMEM_LIMIT = 48 * 1024 * 1024


def face_weights(c):
    a = jnp.abs(c)
    up = c >= 0
    zero = jnp.zeros_like(c)
    edge = c * (1.0 - a) * (1.0 - a)
    far = -c * a * (1.0 - a)
    mid = c * a * (3.0 - 2.0 * a)
    far_p, far_n = jnp.where(up, far, zero), jnp.where(up, zero, far)
    mid_p, mid_n = jnp.where(up, mid, zero), jnp.where(up, zero, mid)
    s, b = 1.0 / 12.0, 7.0 / 12.0
    return [
        -s * far_p,
        b * far_p - s * edge,
        b * (edge + far_p) - s * far_n + mid_p,
        b * (edge + far_n) - s * far_p + mid_n,
        b * far_n - s * edge,
        -s * far_n,
    ]


def cell_weights(west, east):
    out = []
    for k in range(-3, 4):
        total = None
        if k <= 2:
            total = west[k + 3]
        if k >= -2:
            total = -east[k + 2] if total is None else total - east[k + 2]
        out.append(total + 1.0 if k == 0 else total)
    return out


def wall_weights(c):
    lane = lax.broadcasted_iota(jnp.int32, c.shape, 1)
    last = NY - 1
    c = jnp.where(lane == 0, 0.0, c)
    west = face_weights(c)
    east = [pltpu.roll(a, NY - 1, 1) for a in west]
    b = cell_weights(west, east)
    zero = jnp.zeros_like(c)
    m1, m2, m3 = b[2], b[1], b[0]
    p1, p2, p3 = b[4], b[5], b[6]
    low, high = m2 + m3, p2 + p3
    return [
        jnp.where(lane <= 2, zero, m3),
        jnp.where(lane <= 1, zero, jnp.where(lane == 2, low, m2)),
        jnp.where(lane == 0, zero, jnp.where(lane == 1, m1 + low, m1)),
        b[3] + jnp.where(lane == 0, m1 + low, zero) + jnp.where(lane == last, p1 + high, zero),
        jnp.where(lane == last, zero, jnp.where(lane == last - 1, p1 + high, p1)),
        jnp.where(lane >= last - 1, zero, jnp.where(lane == last - 2, high, p2)),
        jnp.where(lane >= last - 2, zero, p3),
    ]


def merge_kernel(flag, own, other, fields, message):
    take = flag[0] == 1
    fields[...] = jnp.where(take, own[...], other[...])
    for x in range(CX):
        for f in range(2):
            message[pl.ds(f * ROWS + x * LEV, LEV), :] = fields[pl.ds(f * ROWS + x, LEV, stride=CX), :]
        total = None
        for l in range(LEV):
            thickness = fields[pl.ds(3 * ROWS + l * CX + x, 1), :]
            row = thickness * fields[pl.ds((4 + l) * ROWS + x, LEV, stride=CX), :]
            total = row if total is None else total + row
        message[pl.ds(2 * ROWS + x * LEV, LEV), :] = total


def weights_kernel(flag, own, first, second, fields, tracers, wx, wy, masses):
    left_first = flag[0] == 1

    def column(f, x):
        rows = pl.ds(f * ROWS + (x % CX) * LEV, LEV)
        if 0 <= x < CX:
            return own[rows, :]
        a, b = first[rows, :], second[rows, :]
        return jnp.where(left_first, a, b) if x < 0 else jnp.where(left_first, b, a)

    w = {x: column(2, x) for x in range(-6, 12)}
    face = {x: face_weights(0.5 * column(0, x)) for x in range(-5, 12)}
    stride = WIDE * 8

    def adjoint_x(v, lo, hi):
        jump = {f: v[f] - v[f - 1] for f in range(lo - 2, hi + 3)}
        out = {}
        for j in range(lo, hi):
            total = v[j]
            for k in range(-3, 3):
                total = total + face[j - k][k + 3] * jump[j - k]
            out[j] = total
        return out

    v = adjoint_x(w, -HALO, CX + HALO)
    for x in range(-HALO, CX + HALO):
        for k, b in enumerate(cell_weights(face[x], face[x + 1])):
            wx[pl.ds((x + HALO) * 8 + k, LEV, stride=stride), :] = b
        b = wall_weights(column(1, x))
        total = None
        for k in range(7):
            wy[pl.ds((x + HALO) * 8 + k, LEV, stride=stride), :] = b[k]
            part = b[k] * v[x]
            if k != 3:
                part = pltpu.roll(part, (k - 3) % NY, 1)
            total = part if total is None else total + part
        v[x] = total
    v = adjoint_x(v, 0, CX)

    before = after = None
    for l in range(LEV):
        for x in range(CX):
            q = tracers[l, x]
            b = q * fields[pl.ds(2 * ROWS + l * CX + x, 1), :]
            a = q * v[x][l : l + 1, :]
            before = b if before is None else before + b
            after = a if after is None else after + a
    both = jnp.concatenate([before, after], axis=0)
    sums = lax.dot_general(
        jnp.ones((8, NY), F32), both, (((1,), (1,)), ((), ())), precision=lax.Precision.HIGHEST, preferred_element_type=F32
    )
    for i in range(masses.shape[0] // 8):
        masses[pl.ds(8 * i, 8), :] = sums


def sweep_kernel(flag, tracers, first, second, wx, wy, fields, received, out, wide, middle, third, sems):
    count = tracers.shape[2]
    left_first = flag[0]
    first_at = (1 - left_first) * 2 * CX
    second_at = left_first * 2 * CX

    def copies(l):
        return [
            pltpu.make_async_copy(tracers.at[l], wide.at[l, pl.ds(CX, CX)], sems.at[l, 0]),
            pltpu.make_async_copy(first.at[l], wide.at[l, pl.ds(first_at, CX)], sems.at[l, 1]),
            pltpu.make_async_copy(second.at[l], wide.at[l, pl.ds(second_at, CX)], sems.at[l, 2]),
        ]

    for l in range(LEV):
        for copy in copies(l):
            copy.start()

    total = jnp.sum(received[...], axis=0, keepdims=True)
    ratio = total / pltpu.roll(jnp.broadcast_to(total, (8, NY)), NY // 2, 1)[:1]
    lane = lax.broadcasted_iota(jnp.int32, (count, NY), 1)
    row = lax.broadcasted_iota(jnp.int32, (count, NY), 0)
    scale = jnp.sum(jnp.where(lane == row, jnp.broadcast_to(ratio, (count, NY)), 0.0), axis=1, keepdims=True)

    block = 32

    def level(l, carry):
        for copy in copies(l):
            copy.wait()
        for t in range(0, count, block):
            ts = pl.ds(t, block)
            for x in range(WIDE):
                value = None
                for k in range(7):
                    part = wx[l, x, pl.ds(k, 1), :] * wide[l, x + k, ts, :]
                    value = part if value is None else value + part
                moved = None
                for k in range(7):
                    q = value if k == 3 else pltpu.roll(value, (3 - k) % NY, 1)
                    part = wy[l, x, pl.ds(k, 1), :] * q
                    moved = part if moved is None else moved + part
                middle[x, ts, :] = moved
            for x in range(CX):
                value = None
                for k in range(7):
                    part = wx[l, x + HALO, pl.ds(k, 1), :] * middle[x + k, ts, :]
                    value = part if value is None else value + part
                third[l, x, ts, :] = value
        return carry

    lax.fori_loop(0, LEV, level, 0)
    for x in range(CX):
        for t in range(0, count, block):
            ts = pl.ds(t, block)
            levels = [third[m, x, ts, :] for m in range(LEV)]
            factor = scale[t : t + block]
            for l in range(LEV):
                value = None
                for m in range(LEV):
                    part = fields[pl.ds((4 + l) * ROWS + m * CX + x, 1), :] * levels[m]
                    value = part if value is None else value + part
                out[l, x, ts, :] = value * factor


SMEM = pl.BlockSpec(memory_space=pltpu.SMEM)
VMEM = pl.BlockSpec(memory_space=pltpu.VMEM)
ANY = pl.BlockSpec(memory_space=pl.ANY)


def call(kernel, ins, outs, scratch=(), flops=0):
    many = isinstance(outs, list)
    shapes = [jax.ShapeDtypeStruct(s, F32) for s in outs] if many else jax.ShapeDtypeStruct(outs, F32)
    return pl.pallas_call(
        kernel,
        out_shape=shapes,
        in_specs=ins,
        out_specs=[VMEM] * len(outs) if many else VMEM,
        scratch_shapes=list(scratch),
        compiler_params=pltpu.CompilerParams(vmem_limit_bytes=VMEM_LIMIT),
    )


def swap(value, axis, partner):
    n = lax.axis_size(axis)
    return lax.ppermute(value, axis, [(i, partner(i, n)) for i in range(n)])


def even_pairs(i, n):
    return i ^ 1


def odd_pairs(i, n):
    return (i + 1) % n if i % 2 else (i - 1) % n


def per_device(tracers, hour_fields, reader_table):
    cells, mine = lax.axis_index("cells"), lax.axis_index("tracers")
    n = lax.axis_size("cells")
    reader = reader_table[0]
    odd = (cells % 2).astype(jnp.int32)[None]
    state = jnp.transpose(tracers, (1, 2, 0, 3))
    count = state.shape[2]
    raw = hour_fields.reshape(NF * ROWS, NY)

    far = swap(raw, "tracers", lambda i, n: i ^ 2)
    half = jnp.where(reader // 2 == mine // 2, raw, far)
    near = swap(half, "tracers", lambda i, n: i ^ 1)
    same = (reader % 2 == mine % 2).astype(jnp.int32)[None]
    fields, message = call(merge_kernel, [SMEM, VMEM, VMEM], [(NF * ROWS, NY), (3 * ROWS, NY)])(same, half, near)

    m1 = swap(message, "cells", even_pairs)
    m2 = swap(message, "cells", odd_pairs)
    h1 = swap(state, "cells", even_pairs)
    h2 = swap(state, "cells", odd_pairs)

    wx, wy, masses = call(
        weights_kernel,
        [SMEM, VMEM, VMEM, VMEM, VMEM, VMEM],
        [(LEV * WIDE * 8, NY), (LEV * WIDE * 8, NY), (n, 2 * count)],
    )(odd, message, m1, m2, fields, state)
    received = lax.all_to_all(masses, "cells", 0, 0, tiled=True)
    wx, wy = wx.reshape(LEV, WIDE, 8, NY), wy.reshape(LEV, WIDE, 8, NY)
    out = call(
        sweep_kernel,
        [SMEM, ANY, ANY, ANY, VMEM, VMEM, VMEM, VMEM],
        (LEV, CX, count, NY),
        [
            pltpu.VMEM((LEV, 3 * CX, count, NY), F32),
            pltpu.VMEM((WIDE, count, NY), F32),
            pltpu.VMEM((LEV, CX, count, NY), F32),
            pltpu.SemaphoreType.DMA((LEV, 3)),
        ],
    )(odd, state, h1, h2, wx, wy, fields, received)
    return jnp.transpose(out, (2, 0, 1, 3))


def solution(mesh):
    placed = (
        P("tracers", None, "cells", None),
        P("tracers", None, None, "cells", None),
        P("cells"),
    )
    return jax.shard_map(
        per_device,
        mesh=mesh,
        in_specs=placed,
        out_specs=P("tracers", None, "cells", None),
        check_vma=False,
    )
```

```python
import functools

import jax
import jax.numpy as jnp
from jax import lax
from jax.experimental import pallas as pl
from jax.experimental.pallas import tpu as pltpu
from jax.sharding import PartitionSpec as P

LEV, CX, NY = 6, 6, 128
ROWS = LEV * CX
NF = 10
HALO = 3
WIDE = CX + 2 * HALO
EARLY = 2
F32 = jnp.float32
VMEM_LIMIT = 10 * 1024 * 1024
WHOLE_VMEM = 60 * 1024 * 1024


def face_weights(c):
    a = jnp.abs(c)
    up = c >= 0
    zero = jnp.zeros_like(c)
    edge = c * (1.0 - a) * (1.0 - a)
    far = -c * a * (1.0 - a)
    mid = c * a * (3.0 - 2.0 * a)
    far_p, far_n = jnp.where(up, far, zero), jnp.where(up, zero, far)
    mid_p, mid_n = jnp.where(up, mid, zero), jnp.where(up, zero, mid)
    s, b = 1.0 / 12.0, 7.0 / 12.0
    return [
        -s * far_p,
        b * far_p - s * edge,
        b * (edge + far_p) - s * far_n + mid_p,
        b * (edge + far_n) - s * far_p + mid_n,
        b * far_n - s * edge,
        -s * far_n,
    ]


def cell_weights(west, east):
    out = []
    for k in range(-3, 4):
        total = None
        if k <= 2:
            total = west[k + 3]
        if k >= -2:
            total = -east[k + 2] if total is None else total - east[k + 2]
        out.append(total + 1.0 if k == 0 else total)
    return out


def wall_weights(c):
    lane = lax.broadcasted_iota(jnp.int32, c.shape, 1)
    last = NY - 1
    c = jnp.where(lane == 0, 0.0, c)
    west = face_weights(c)
    east = [pltpu.roll(a, NY - 1, 1) for a in west]
    b = cell_weights(west, east)
    zero = jnp.zeros_like(c)
    m1, m2, m3 = b[2], b[1], b[0]
    p1, p2, p3 = b[4], b[5], b[6]
    low, high = m2 + m3, p2 + p3
    return [
        jnp.where(lane <= 2, zero, m3),
        jnp.where(lane <= 1, zero, jnp.where(lane == 2, low, m2)),
        jnp.where(lane == 0, zero, jnp.where(lane == 1, m1 + low, m1)),
        b[3] + jnp.where(lane == 0, m1 + low, zero) + jnp.where(lane == last, p1 + high, zero),
        jnp.where(lane == last, zero, jnp.where(lane == last - 1, p1 + high, p1)),
        jnp.where(lane >= last - 1, zero, jnp.where(lane == last - 2, high, p2)),
        jnp.where(lane >= last - 2, zero, p3),
    ]


def split_kernel(start, tracers, *rest):
    part, sems = rest[-2:]
    moves = [pltpu.make_async_copy(tracers.at[start + l], part.at[l], sems.at[l]) for l in range(part.shape[0])]
    for move in moves:
        move.start()
    for move in moves:
        move.wait()


def gate_kernel(*refs):
    pass


def merge_kernel(place, own, near, far, across, fields, message):
    core, chip = place[0] == 1, place[1] == 1
    here = jnp.where(core, own[...], near[...])
    there = jnp.where(core, far[...], across[...])
    fields[...] = jnp.where(chip, here, there)
    for x in range(CX):
        for f in range(2):
            message[pl.ds(f * ROWS + x * LEV, LEV), :] = fields[pl.ds(f * ROWS + x, LEV, stride=CX), :]
        total = None
        for l in range(LEV):
            thickness = fields[pl.ds(3 * ROWS + l * CX + x, 1), :]
            row = thickness * fields[pl.ds((4 + l) * ROWS + x, LEV, stride=CX), :]
            total = row if total is None else total + row
        message[pl.ds(2 * ROWS + x * LEV, LEV), :] = total


def weights_kernel(flag, own, first, second, fields, tracers, wx, wy, masses):
    left_first = flag[0] == 1

    def column(f, x):
        rows = pl.ds(f * ROWS + (x % CX) * LEV, LEV)
        if 0 <= x < CX:
            return own[rows, :]
        a, b = first[rows, :], second[rows, :]
        return jnp.where(left_first, a, b) if x < 0 else jnp.where(left_first, b, a)

    w = {x: column(2, x) for x in range(-6, 12)}
    face = {x: face_weights(0.5 * column(0, x)) for x in range(-5, 12)}
    stride = WIDE * 8

    def adjoint_x(v, lo, hi):
        jump = {f: v[f] - v[f - 1] for f in range(lo - 2, hi + 3)}
        out = {}
        for j in range(lo, hi):
            total = v[j]
            for k in range(-3, 3):
                total = total + face[j - k][k + 3] * jump[j - k]
            out[j] = total
        return out

    v = adjoint_x(w, -HALO, CX + HALO)
    for x in range(-HALO, CX + HALO):
        for k, b in enumerate(cell_weights(face[x], face[x + 1])):
            wx[pl.ds((x + HALO) * 8 + k, LEV, stride=stride), :] = b
        b = wall_weights(column(1, x))
        total = None
        for k in range(7):
            wy[pl.ds((x + HALO) * 8 + k, LEV, stride=stride), :] = b[k]
            part = b[k] * v[x]
            if k != 3:
                part = pltpu.roll(part, (k - 3) % NY, 1)
            total = part if total is None else total + part
        v[x] = total
    v = adjoint_x(v, 0, CX)

    before = after = None
    for l in range(LEV):
        for x in range(CX):
            q = tracers[l, x]
            b = q * fields[pl.ds(2 * ROWS + l * CX + x, 1), :]
            a = q * v[x][l : l + 1, :]
            before = b if before is None else before + b
            after = a if after is None else after + a
    both = jnp.concatenate([before, after], axis=0)
    sums = lax.dot_general(
        jnp.ones((8, NY), F32), both, (((1,), (1,)), ((), ())), precision=lax.Precision.HIGHEST, preferred_element_type=F32
    )
    for i in range(masses.shape[0] // 8):
        masses[pl.ds(8 * i, 8), :] = sums


def start_wide(flag, start, tracers, first, second, wide, sems):
    first_at = (1 - flag[0]) * 2 * CX
    second_at = flag[0] * 2 * CX

    def copies(l):
        return [
            pltpu.make_async_copy(tracers.at[start + l], wide.at[l, pl.ds(CX, CX)], sems.at[l, 0]),
            pltpu.make_async_copy(first.at[l], wide.at[l, pl.ds(first_at, CX)], sems.at[l, 1]),
            pltpu.make_async_copy(second.at[l], wide.at[l, pl.ds(second_at, CX)], sems.at[l, 2]),
        ]

    for l in range(first.shape[0]):
        for copy in copies(l):
            copy.start()
    return copies


def sweep_levels(start, copies, wide, wx, wy, middle, third, third_at):
    count, block = middle.shape[1], 32

    def level(l, carry):
        for copy in copies(l):
            copy.wait()
        row = (start + l) * WIDE

        def weight(ref, x, k):
            return ref[pl.ds((row + x) * 8 + k, 1), :]

        for t in range(0, count, block):
            ts = pl.ds(t, block)
            for x in range(WIDE):
                value = None
                for k in range(7):
                    part = weight(wx, x, k) * wide[l, x + k, ts, :]
                    value = part if value is None else value + part
                moved = None
                for k in range(7):
                    q = value if k == 3 else pltpu.roll(value, (3 - k) % NY, 1)
                    part = weight(wy, x, k) * q
                    moved = part if moved is None else moved + part
                middle[x, ts, :] = moved
            for x in range(CX):
                value = None
                for k in range(7):
                    part = weight(wx, x + HALO, k) * middle[x + k, ts, :]
                    value = part if value is None else value + part
                third[third_at + l, x, ts, :] = value
        return carry

    lax.fori_loop(0, wide.shape[0], level, 0)


def early_kernel(flag, tracers, h1, h2, wx, wy, third, wide, middle, sems):
    copies = start_wide(flag, 0, tracers, h1, h2, wide, sems)
    sweep_levels(0, copies, wide, wx, wy, middle, third, 0)


def late_kernel(flag, tracers, h1, h2, wx, wy, fields, early, out, wide, middle, third, sems):
    done = early.shape[0]
    copies = start_wide(flag, done, tracers, h1, h2, wide, sems)
    count, block = tracers.shape[2], 32
    sweep_levels(done, copies, wide, wx, wy, middle, third, 0)
    for x in range(CX):
        for t in range(0, count, block):
            ts = pl.ds(t, block)
            levels = [early[m, x, ts, :] if m < done else third[m - done, x, ts, :] for m in range(LEV)]
            for l in range(LEV):
                value = None
                for m in range(LEV):
                    part = fields[pl.ds((4 + l) * ROWS + m * CX + x, 1), :] * levels[m]
                    value = part if value is None else value + part
                out[l, x, ts, :] = value


def scale_kernel(received, diffused, out, scaled, sems):
    count = diffused.shape[2]
    total = jnp.sum(received[...], axis=0, keepdims=True)
    ratio = total / pltpu.roll(jnp.broadcast_to(total, (8, NY)), NY // 2, 1)[:1]
    lane = lax.broadcasted_iota(jnp.int32, (count, NY), 1)
    row = lax.broadcasted_iota(jnp.int32, (count, NY), 0)
    scale = jnp.sum(jnp.where(lane == row, jnp.broadcast_to(ratio, (count, NY)), 0.0), axis=1, keepdims=True)
    factor = jnp.broadcast_to(scale, (count, NY))
    moves = [pltpu.make_async_copy(scaled.at[l], out.at[l], sems.at[l]) for l in range(LEV)]
    for l in range(LEV):
        for x in range(CX):
            scaled[l, x] = diffused[l, x] * factor
        moves[l].start()
    for move in moves:
        move.wait()


SMEM = pl.BlockSpec(memory_space=pltpu.SMEM)
VMEM = pl.BlockSpec(memory_space=pltpu.VMEM)
ANY = pl.BlockSpec(memory_space=pl.ANY)
HBM = pl.BlockSpec(memory_space=pltpu.HBM)


def call(kernel, ins, outs, places=None, scratch=(), limit=VMEM_LIMIT, aliases=()):
    return pl.pallas_call(
        kernel,
        out_shape=[jax.ShapeDtypeStruct(s, F32) for s in outs],
        in_specs=ins,
        out_specs=places or [VMEM] * len(outs),
        scratch_shapes=list(scratch),
        compiler_params=pltpu.CompilerParams(vmem_limit_bytes=limit),
        input_output_aliases=dict(aliases),
    )


def swap(value, axis, partner):
    n = lax.axis_size(axis)
    return lax.ppermute(value, axis, [(i, partner(i, n)) for i in range(n)])


def even_pairs(i, n):
    return i ^ 1


def odd_pairs(i, n):
    return (i + 1) % n if i % 2 else (i - 1) % n


def per_device(tracers, hour_fields, reader_table):
    cells, mine = lax.axis_index("cells"), lax.axis_index("tracers")
    n = lax.axis_size("cells")
    reader = reader_table[0]
    odd = (cells % 2).astype(jnp.int32)[None]
    state = jnp.transpose(tracers, (1, 2, 0, 3))
    count = state.shape[2]
    raw = hour_fields.reshape(NF * ROWS, NY)

    early, late = EARLY, LEV - EARLY

    def other_core(value):
        return swap(value, "tracers", lambda i, n: i ^ 1)

    far = swap(raw, "tracers", lambda i, n: i ^ 2)
    near = other_core(raw)
    def split(start, levels, after, limit, place):
        kernel = functools.partial(split_kernel, start)
        ins, shape = [HBM] + [ANY] * len(after), (levels, CX, count, NY)
        return call(kernel, ins, [shape], [place], [pltpu.SemaphoreType.DMA((levels,))], limit)(state, *after)[0]

    chunk = split(0, early, [], VMEM_LIMIT, ANY)
    a2 = swap(chunk, "cells", odd_pairs)
    a1 = swap(chunk, "cells", even_pairs)
    across = other_core(far)
    place = jnp.stack([reader % 2 == mine % 2, reader // 2 == mine // 2]).astype(jnp.int32)
    fields, message = call(
        merge_kernel, [SMEM, VMEM, VMEM, VMEM, VMEM], [(NF * ROWS, NY), (3 * ROWS, NY)]
    )(place, raw, near, far, across)

    m1 = swap(message, "cells", even_pairs)
    m2 = swap(message, "cells", odd_pairs)
    rest = split(early, late, [far], VMEM_LIMIT, ANY)
    rest = call(gate_kernel, [ANY] * 5, [rest.shape], [ANY], aliases={0: 0})(rest, m1, m2, a1, a2)[0]
    b1 = swap(rest, "cells", even_pairs)
    b2 = swap(rest, "cells", odd_pairs)

    wx, wy, masses = call(
        weights_kernel,
        [SMEM, VMEM, VMEM, VMEM, VMEM, VMEM],
        [(LEV * WIDE * 8, NY), (LEV * WIDE * 8, NY), (n, 2 * count)],
    )(odd, message, m1, m2, fields, state)
    received = lax.all_to_all(masses, "cells", 0, 0, tiled=True)
    third = call(
        early_kernel,
        [SMEM, ANY, ANY, ANY, VMEM, VMEM],
        [(early, CX, count, NY)],
        None,
        [
            pltpu.VMEM((early, 3 * CX, count, NY), F32),
            pltpu.VMEM((WIDE, count, NY), F32),
            pltpu.SemaphoreType.DMA((early, 3)),
        ],
    )(odd, state, a1, a2, wx, wy)[0]
    diffused = call(
        late_kernel,
        [SMEM, ANY, ANY, ANY, VMEM, VMEM, VMEM, VMEM],
        [(LEV, CX, count, NY)],
        None,
        [
            pltpu.VMEM((late, 3 * CX, count, NY), F32),
            pltpu.VMEM((WIDE, count, NY), F32),
            pltpu.VMEM((late, CX, count, NY), F32),
            pltpu.SemaphoreType.DMA((late, 3)),
        ],
    )(odd, state, b1, b2, wx, wy, fields, third)[0]
    out = call(
        scale_kernel,
        [VMEM, VMEM],
        [(LEV, CX, count, NY)],
        [HBM],
        [pltpu.VMEM((LEV, CX, count, NY), F32), pltpu.SemaphoreType.DMA((LEV,))],
    )(received, diffused)[0]
    return jnp.transpose(out, (2, 0, 1, 3))


def solution(mesh):
    placed = (
        P("tracers", None, "cells", None),
        P("tracers", None, None, "cells", None),
        P("cells"),
    )
    return jax.shard_map(
        per_device,
        mesh=mesh,
        in_specs=placed,
        out_specs=P("tracers", None, "cells", None),
        check_vma=False,
    )
```

```python
import functools

import jax
import jax.numpy as jnp
from jax import lax
from jax.experimental import pallas as pl
from jax.experimental.pallas import tpu as pltpu
from jax.sharding import PartitionSpec as P

LEV, CX, NY = 6, 6, 128
ROWS = LEV * CX
NF = 10
HALO = 3
WIDE = CX + 2 * HALO
CHUNKS = (2, 0)
KA_FLOPS = 10000000000
KB_FLOPS = 0
MERGE_FLOPS = 0
HEAD = 112
F32 = jnp.float32
VMEM_LIMIT = 10 * 1024 * 1024


def face_weights(c):
    a = jnp.abs(c)
    up = c >= 0
    zero = jnp.zeros_like(c)
    edge = c * (1.0 - a) * (1.0 - a)
    far = -c * a * (1.0 - a)
    mid = c * a * (3.0 - 2.0 * a)
    far_p, far_n = jnp.where(up, far, zero), jnp.where(up, zero, far)
    mid_p, mid_n = jnp.where(up, mid, zero), jnp.where(up, zero, mid)
    s, b = 1.0 / 12.0, 7.0 / 12.0
    return [
        -s * far_p,
        b * far_p - s * edge,
        b * (edge + far_p) - s * far_n + mid_p,
        b * (edge + far_n) - s * far_p + mid_n,
        b * far_n - s * edge,
        -s * far_n,
    ]


def cell_weights(west, east):
    out = []
    for k in range(-3, 4):
        total = None
        if k <= 2:
            total = west[k + 3]
        if k >= -2:
            total = -east[k + 2] if total is None else total - east[k + 2]
        out.append(total + 1.0 if k == 0 else total)
    return out


def wall_weights(c):
    lane = lax.broadcasted_iota(jnp.int32, c.shape, 1)
    last = NY - 1
    c = jnp.where(lane == 0, 0.0, c)
    west = face_weights(c)
    east = [pltpu.roll(a, NY - 1, 1) for a in west]
    b = cell_weights(west, east)
    zero = jnp.zeros_like(c)
    m1, m2, m3 = b[2], b[1], b[0]
    p1, p2, p3 = b[4], b[5], b[6]
    low, high = m2 + m3, p2 + p3
    return [
        jnp.where(lane <= 2, zero, m3),
        jnp.where(lane <= 1, zero, jnp.where(lane == 2, low, m2)),
        jnp.where(lane == 0, zero, jnp.where(lane == 1, m1 + low, m1)),
        b[3] + jnp.where(lane == 0, m1 + low, zero) + jnp.where(lane == last, p1 + high, zero),
        jnp.where(lane == last, zero, jnp.where(lane == last - 1, p1 + high, p1)),
        jnp.where(lane >= last - 1, zero, jnp.where(lane == last - 2, high, p2)),
        jnp.where(lane >= last - 2, zero, p3),
    ]


def split_kernel(start, tracers, *rest):
    part, sems = rest[-2:]
    moves = [pltpu.make_async_copy(tracers.at[start + l], part.at[l], sems.at[l]) for l in range(part.shape[0])]
    for move in moves:
        move.start()
    for move in moves:
        move.wait()


def merge_kernel(same_core, same_chip, own, near, far, across, after, fields, message):
    core, chip = same_core[0] == 1, same_chip[0] == 1
    here = jnp.where(core, own[...], near[...])
    there = jnp.where(core, far[...], across[...])
    fields[...] = jnp.where(chip, here, there)
    for x in range(CX):
        for f in range(2):
            message[pl.ds(f * ROWS + x * LEV, LEV), :] = fields[pl.ds(f * ROWS + x, LEV, stride=CX), :]
        total = None
        for l in range(LEV):
            thickness = fields[pl.ds(3 * ROWS + l * CX + x, 1), :]
            row = thickness * fields[pl.ds((4 + l) * ROWS + x, LEV, stride=CX), :]
            total = row if total is None else total + row
        message[pl.ds(2 * ROWS + x * LEV, LEV), :] = total


def weights_kernel(flag, own, first, second, fields, tracers, after, wx, wy, masses):
    left_first = flag[0] == 1

    def column(f, x):
        rows = pl.ds(f * ROWS + (x % CX) * LEV, LEV)
        if 0 <= x < CX:
            return own[rows, :]
        a, b = first[rows, :], second[rows, :]
        return jnp.where(left_first, a, b) if x < 0 else jnp.where(left_first, b, a)

    w = {x: column(2, x) for x in range(-6, 12)}
    face = {x: face_weights(0.5 * column(0, x)) for x in range(-5, 12)}
    stride = WIDE * 8

    def adjoint_x(v, lo, hi):
        jump = {f: v[f] - v[f - 1] for f in range(lo - 2, hi + 3)}
        out = {}
        for j in range(lo, hi):
            total = v[j]
            for k in range(-3, 3):
                total = total + face[j - k][k + 3] * jump[j - k]
            out[j] = total
        return out

    v = adjoint_x(w, -HALO, CX + HALO)
    for x in range(-HALO, CX + HALO):
        for k, b in enumerate(cell_weights(face[x], face[x + 1])):
            wx[pl.ds((x + HALO) * 8 + k, LEV, stride=stride), :] = b
        b = wall_weights(column(1, x))
        total = None
        for k in range(7):
            wy[pl.ds((x + HALO) * 8 + k, LEV, stride=stride), :] = b[k]
            part = b[k] * v[x]
            if k != 3:
                part = pltpu.roll(part, (k - 3) % NY, 1)
            total = part if total is None else total + part
        v[x] = total
    v = adjoint_x(v, 0, CX)

    before = after = None
    for l in range(LEV):
        for x in range(CX):
            q = tracers[l, x]
            b = q * fields[pl.ds(2 * ROWS + l * CX + x, 1), :]
            a = q * v[x][l : l + 1, :]
            before = b if before is None else before + b
            after = a if after is None else after + a
    both = jnp.concatenate([before, after], axis=0)
    sums = lax.dot_general(
        jnp.ones((8, NY), F32), both, (((1,), (1,)), ((), ())), precision=lax.Precision.HIGHEST, preferred_element_type=F32
    )
    for i in range(masses.shape[0] // 8):
        masses[pl.ds(8 * i, 8), :] = sums


def start_wide(flag, start, tracers, first, second, wide, sems):
    size = tracers.shape[1]
    first_at = (1 - flag[0]) * 2 * size
    second_at = flag[0] * 2 * size

    def level(ref, l):
        return ref.at[l] if ref.ndim == 3 else ref.at[pl.ds(pl.multiple_of(HEAD + l * size, 8), size)]

    def copies(l):
        return [
            pltpu.make_async_copy(tracers.at[start + l], wide.at[l, pl.ds(size, size)], sems.at[l, 0]),
            pltpu.make_async_copy(level(first, l), wide.at[l, pl.ds(first_at, size)], sems.at[l, 1]),
            pltpu.make_async_copy(level(second, l), wide.at[l, pl.ds(second_at, size)], sems.at[l, 2]),
        ]

    for l in range(wide.shape[0]):
        for copy in copies(l):
            copy.start()
    return copies


def sweep_levels(start, copies, wide, wx, wy, middle, third, third_at):
    count, block = middle.shape[1], 32

    def column(l, x, t):
        if not isinstance(wide, tuple):
            return wide[l, pl.ds(x * count + t, block), :]
        return wide[x // CX][l + (start if x // CX == 1 else 0), pl.ds(x % CX * count + t, block), :]

    def level(l, carry):
        for copy in copies(l) if copies else ():
            copy.wait()
        row = (start + l) * WIDE

        def weight(ref, x, k):
            return ref[pl.ds((row + x) * 8 + k, 1), :]

        for t in range(0, count, block):
            ts = pl.ds(t, block)
            for x in range(WIDE):
                value = None
                for k in range(7):
                    part = weight(wx, x, k) * column(l, x + k, t)
                    value = part if value is None else value + part
                moved = None
                for k in range(7):
                    q = value if k == 3 else pltpu.roll(value, (3 - k) % NY, 1)
                    part = weight(wy, x, k) * q
                    moved = part if moved is None else moved + part
                middle[x, ts, :] = moved
            for x in range(CX):
                value = None
                for k in range(7):
                    part = weight(wx, x + HALO, k) * middle[x + k, ts, :]
                    value = part if value is None else value + part
                third[third_at + l, x, ts, :] = value
        return carry

    lax.fori_loop(0, wide[0].shape[0] if isinstance(wide, tuple) else wide.shape[0], level, 0)


def token_kernel(first, second, token):
    token[...] = jnp.zeros_like(token)


def gate_kernel(*refs):
    pass


def early_kernel(flag, tracers, h1, h2, wx, wy, third, wide, middle, sems):
    copies = start_wide(flag, 0, tracers, h1, h2, wide, sems)
    sweep_levels(0, copies, wide, wx, wy, middle, third, 0)


def late_kernel(flag, tracers, h1, h2, wx, wy, fields, early, out, middle, third):
    done, count, block = early.shape[0], early.shape[2], 32

    @pl.when(flag[0] == 1)
    def _():
        sweep_levels(done, None, (h1, tracers, h2), wx, wy, middle, third, 0)

    @pl.when(flag[0] == 0)
    def _():
        sweep_levels(done, None, (h2, tracers, h1), wx, wy, middle, third, 0)

    for x in range(CX):
        for t in range(0, count, block):
            ts = pl.ds(t, block)
            levels = [early[m, x, ts, :] if m < done else third[m - done, x, ts, :] for m in range(LEV)]
            for l in range(LEV):
                value = None
                for m in range(LEV):
                    part = fields[pl.ds((4 + l) * ROWS + m * CX + x, 1), :] * levels[m]
                    value = part if value is None else value + part
                out[l, x, ts, :] = value


def scale_kernel(received, diffused, out, scaled, sems):
    count = diffused.shape[2]
    total = jnp.sum(received[...], axis=0, keepdims=True)
    ratio = total / pltpu.roll(jnp.broadcast_to(total, (8, NY)), NY // 2, 1)[:1]
    lane = lax.broadcasted_iota(jnp.int32, (count, NY), 1)
    row = lax.broadcasted_iota(jnp.int32, (count, NY), 0)
    scale = jnp.sum(jnp.where(lane == row, jnp.broadcast_to(ratio, (count, NY)), 0.0), axis=1, keepdims=True)
    factor = jnp.broadcast_to(scale, (count, NY))
    moves = [pltpu.make_async_copy(scaled.at[l], out.at[l], sems.at[l]) for l in range(LEV)]
    for l in range(LEV):
        for x in range(CX):
            scaled[l, x] = diffused[l, x] * factor
        moves[l].start()
    for move in moves:
        move.wait()


SMEM = pl.BlockSpec(memory_space=pltpu.SMEM)
VMEM = pl.BlockSpec(memory_space=pltpu.VMEM)
ANY = pl.BlockSpec(memory_space=pl.ANY)
HBM = pl.BlockSpec(memory_space=pltpu.HBM)


def work(flops):
    return pl.CostEstimate(flops=flops, bytes_accessed=0, transcendentals=0)


def call(kernel, ins, outs, places=None, scratch=(), limit=VMEM_LIMIT, aliases=(), cost=None):
    places = places or [VMEM] * len(outs)
    return pl.pallas_call(
        kernel,
        out_shape=[s if not isinstance(s, tuple) else pltpu.VMEM(s, F32) if p is VMEM else jax.ShapeDtypeStruct(s, F32) for s, p in zip(outs, places)],
        in_specs=ins,
        out_specs=places,
        scratch_shapes=list(scratch),
        compiler_params=pltpu.CompilerParams(vmem_limit_bytes=limit),
        input_output_aliases=dict(aliases),
        cost_estimate=cost,
    )


def in_hbm(value):
    return pltpu.with_memory_space_constraint(value, pltpu.HBM)


def in_vmem(value):
    return pltpu.with_memory_space_constraint(value, pltpu.VMEM)


def swap(value, axis, partner):
    n = lax.axis_size(axis)
    return lax.ppermute(value, axis, [(i, partner(i, n)) for i in range(n)])


def even_pairs(i, n):
    return i ^ 1


def odd_pairs(i, n):
    return (i + 1) % n if i % 2 else (i - 1) % n


def per_device(tracers, hour_fields, reader_table):
    cells, mine = lax.axis_index("cells"), lax.axis_index("tracers")
    n = lax.axis_size("cells")
    reader = reader_table[0]
    odd = (cells % 2).astype(jnp.int32)[None]
    state = jnp.transpose(tracers, (1, 2, 0, 3))
    count = state.shape[2]
    raw = hour_fields.reshape(NF * ROWS, NY)

    a_levels, c_levels = CHUNKS
    early, late = a_levels + c_levels, LEV - a_levels - c_levels
    flat = state.reshape(LEV, CX * count, NY)

    def other_core(value):
        return swap(value, "tracers", lambda i, n: i ^ 1)

    far = swap(raw, "tracers", lambda i, n: i ^ 2)
    near = other_core(raw)
    def split(start, levels, *after):
        kernel = functools.partial(split_kernel, start)
        shape = (levels, CX * count, NY)
        return call(kernel, [ANY] * (1 + len(after)), [shape], [ANY], [pltpu.SemaphoreType.DMA((levels,))])(in_hbm(flat), *after)[0]

    chunk = split(0, a_levels)
    a1 = swap(chunk, "cells", even_pairs)
    a2 = swap(chunk, "cells", odd_pairs)
    across = other_core(far)
    same_core = (reader % 2 == mine % 2).astype(jnp.int32)[None]
    same_chip = (reader // 2 == mine // 2).astype(jnp.int32)[None]
    rest = split(early, late, far)
    fields, message = call(merge_kernel, [SMEM, SMEM, VMEM, VMEM, VMEM, VMEM, ANY], [(NF * ROWS, NY), (3 * ROWS, NY)], cost=work(MERGE_FLOPS))(
        same_core, same_chip, raw, near, far, across, rest
    )
    c1 = swap(message, "cells", even_pairs)
    c2 = swap(message, "cells", odd_pairs)
    rest = call(gate_kernel, [ANY, ANY], [rest.shape], [ANY], aliases={0: 0})(rest, message)[0]
    b1 = swap(rest, "cells", even_pairs)
    b2 = swap(rest, "cells", odd_pairs)

    token = call(token_kernel, [ANY, ANY], [(8, NY)])(in_hbm(a1), in_hbm(a2))[0]
    wx, wy, masses = call(
        weights_kernel,
        [SMEM, VMEM, VMEM, VMEM, VMEM, VMEM, ANY],
        [pltpu.HBM((LEV * WIDE * 8, NY), F32), pltpu.HBM((LEV * WIDE * 8, NY), F32), (n, 2 * count)],
    )(odd, message, c1, c2, fields, state, token)
    received = lax.all_to_all(masses, "cells", 0, 0, tiled=True)
    third = call(
        early_kernel,
        [SMEM, ANY, ANY, ANY, VMEM, VMEM],
        [(early, CX, count, NY)],
        None,
        [
            pltpu.VMEM((early, 3 * CX * count, NY), F32),
            pltpu.VMEM((WIDE, count, NY), F32),
            pltpu.SemaphoreType.DMA((early, 3)),
        ],
        cost=work(KA_FLOPS),
    )(odd, flat, in_hbm(a1), in_hbm(a2), wx, wy)[0]
    diffused = call(
        late_kernel,
        [SMEM] + [VMEM] * 7,
        [(LEV, CX, count, NY)],
        None,
        [
            pltpu.VMEM((WIDE, count, NY), F32),
            pltpu.VMEM((late, CX, count, NY), F32),
        ],
        cost=work(KB_FLOPS),
    )(odd, flat, in_vmem(b1), in_vmem(b2), wx, wy, fields, third)[0]
    out = call(
        scale_kernel,
        [VMEM, VMEM],
        [(LEV, CX, count, NY)],
        [HBM],
        [pltpu.VMEM((LEV, CX, count, NY), F32), pltpu.SemaphoreType.DMA((LEV,))],
    )(received, diffused)[0]
    return jnp.transpose(out, (2, 0, 1, 3))


def solution(mesh):
    placed = (
        P("tracers", None, "cells", None),
        P("tracers", None, None, "cells", None),
        P("cells"),
    )
    return jax.shard_map(
        per_device,
        mesh=mesh,
        in_specs=placed,
        out_specs=P("tracers", None, "cells", None),
        check_vma=False,
    )
```

```python
import functools

import jax
import jax.numpy as jnp
from jax import lax
from jax.experimental import pallas as pl
from jax.experimental.pallas import tpu as pltpu
from jax.sharding import PartitionSpec as P

LEV, CX, NY = 6, 6, 128
ROWS = LEV * CX
NF = 10
HALO = 3
WIDE = CX + 2 * HALO
CHUNKS = (2, 0)
KA_FLOPS = 10000000000
KB_FLOPS = 0
MERGE_FLOPS = 0
HEAD = 112
F32 = jnp.float32
VMEM_LIMIT = 10 * 1024 * 1024


def face_weights(c):
    a = jnp.abs(c)
    up = c >= 0
    zero = jnp.zeros_like(c)
    edge = c * (1.0 - a) * (1.0 - a)
    far = -c * a * (1.0 - a)
    mid = c * a * (3.0 - 2.0 * a)
    far_p, far_n = jnp.where(up, far, zero), jnp.where(up, zero, far)
    mid_p, mid_n = jnp.where(up, mid, zero), jnp.where(up, zero, mid)
    s, b = 1.0 / 12.0, 7.0 / 12.0
    return [
        -s * far_p,
        b * far_p - s * edge,
        b * (edge + far_p) - s * far_n + mid_p,
        b * (edge + far_n) - s * far_p + mid_n,
        b * far_n - s * edge,
        -s * far_n,
    ]


def cell_weights(west, east):
    out = []
    for k in range(-3, 4):
        total = None
        if k <= 2:
            total = west[k + 3]
        if k >= -2:
            total = -east[k + 2] if total is None else total - east[k + 2]
        out.append(total + 1.0 if k == 0 else total)
    return out


def wall_weights(c):
    lane = lax.broadcasted_iota(jnp.int32, c.shape, 1)
    last = NY - 1
    c = jnp.where(lane == 0, 0.0, c)
    west = face_weights(c)
    east = [pltpu.roll(a, NY - 1, 1) for a in west]
    b = cell_weights(west, east)
    zero = jnp.zeros_like(c)
    m1, m2, m3 = b[2], b[1], b[0]
    p1, p2, p3 = b[4], b[5], b[6]
    low, high = m2 + m3, p2 + p3
    return [
        jnp.where(lane <= 2, zero, m3),
        jnp.where(lane <= 1, zero, jnp.where(lane == 2, low, m2)),
        jnp.where(lane == 0, zero, jnp.where(lane == 1, m1 + low, m1)),
        b[3] + jnp.where(lane == 0, m1 + low, zero) + jnp.where(lane == last, p1 + high, zero),
        jnp.where(lane == last, zero, jnp.where(lane == last - 1, p1 + high, p1)),
        jnp.where(lane >= last - 1, zero, jnp.where(lane == last - 2, high, p2)),
        jnp.where(lane >= last - 2, zero, p3),
    ]


def split_kernel(start, tracers, part, sems):
    moves = [pltpu.make_async_copy(tracers.at[start + l], part.at[l], sems.at[l]) for l in range(part.shape[0])]
    for move in moves:
        move.start()
    for move in moves:
        move.wait()


def split_mask_kernel(start, reader, mine, tracers, part, mask, sems):
    differ = reader[0] ^ mine[0]
    mask[pl.ds(0, 8), :] = jnp.full((8, NY), differ & 1, jnp.int32)
    mask[pl.ds(8, 8), :] = jnp.full((8, NY), differ >> 1, jnp.int32)
    split_kernel(start, tracers, part, sems)


def merge_kernel(mask, own, near, far, across, fields, message):
    core, chip = mask[pl.ds(0, 1), :] == 0, mask[pl.ds(8, 1), :] == 0
    here = jnp.where(core, own[...], near[...])
    there = jnp.where(core, far[...], across[...])
    fields[...] = jnp.where(chip, here, there)
    for x in range(CX):
        for f in range(2):
            message[pl.ds(f * ROWS + x * LEV, LEV), :] = fields[pl.ds(f * ROWS + x, LEV, stride=CX), :]
        total = None
        for l in range(LEV):
            thickness = fields[pl.ds(3 * ROWS + l * CX + x, 1), :]
            row = thickness * fields[pl.ds((4 + l) * ROWS + x, LEV, stride=CX), :]
            total = row if total is None else total + row
        message[pl.ds(2 * ROWS + x * LEV, LEV), :] = total


def weights_kernel(flag, own, first, second, fields, tracers, after, wx, wy, masses):
    left_first = flag[0] == 1

    def column(f, x):
        rows = pl.ds(f * ROWS + (x % CX) * LEV, LEV)
        if 0 <= x < CX:
            return own[rows, :]
        a, b = first[rows, :], second[rows, :]
        return jnp.where(left_first, a, b) if x < 0 else jnp.where(left_first, b, a)

    w = {x: column(2, x) for x in range(-6, 12)}
    face = {x: face_weights(0.5 * column(0, x)) for x in range(-5, 12)}
    stride = WIDE * 8

    def adjoint_x(v, lo, hi):
        jump = {f: v[f] - v[f - 1] for f in range(lo - 2, hi + 3)}
        out = {}
        for j in range(lo, hi):
            total = v[j]
            for k in range(-3, 3):
                total = total + face[j - k][k + 3] * jump[j - k]
            out[j] = total
        return out

    v = adjoint_x(w, -HALO, CX + HALO)
    for x in range(-HALO, CX + HALO):
        for k, b in enumerate(cell_weights(face[x], face[x + 1])):
            wx[pl.ds((x + HALO) * 8 + k, LEV, stride=stride), :] = b
        b = wall_weights(column(1, x))
        total = None
        for k in range(7):
            wy[pl.ds((x + HALO) * 8 + k, LEV, stride=stride), :] = b[k]
            part = b[k] * v[x]
            if k != 3:
                part = pltpu.roll(part, (k - 3) % NY, 1)
            total = part if total is None else total + part
        v[x] = total
    v = adjoint_x(v, 0, CX)

    before = after = None
    for l in range(LEV):
        for x in range(CX):
            q = tracers[l, x]
            b = q * fields[pl.ds(2 * ROWS + l * CX + x, 1), :]
            a = q * v[x][l : l + 1, :]
            before = b if before is None else before + b
            after = a if after is None else after + a
    both = jnp.concatenate([before, after], axis=0)
    sums = lax.dot_general(
        jnp.ones((8, NY), F32), both, (((1,), (1,)), ((), ())), precision=lax.Precision.HIGHEST, preferred_element_type=F32
    )
    for i in range(masses.shape[0] // 8):
        masses[pl.ds(8 * i, 8), :] = sums


def stencil(weight, q):
    value = weight(0) * q(0)
    for k in range(1, 7):
        value = value + weight(k) * q(k)
    return value


def sweeps(level, columns, first, last, wx, wy, middle, third):
    count, block = middle.shape[1], 32

    def weights(ref, x):
        return lambda k: ref[pl.ds((level * WIDE + x) * 8 + k, 1), :]

    for t in range(0, count, block):
        ts = pl.ds(t, block)
        for x in range(first, last):
            value = stencil(weights(wx, x), lambda k: columns[(x + k) // CX][pl.ds((x + k) % CX * count + t, block), :])
            middle[x, ts, :] = stencil(weights(wy, x), lambda k: value if k == 3 else pltpu.roll(value, (3 - k) % NY, 1))
        for x in range(CX if third is not None else 0):
            third[x, ts, :] = stencil(weights(wx, x + HALO), lambda k: middle[x + k, ts, :])


def token_kernel(first, second, token):
    token[...] = jnp.zeros_like(token)


def gate_kernel(*refs):
    pass


def early_kernel(flag, tracers, h1, h2, wx, wy, third, s1, s2, middle, sems):
    def copies(l):
        return [pltpu.make_async_copy(h.at[l], s.at[l], sems.at[l, i]) for i, (h, s) in enumerate(((h1, s1), (h2, s2)))]

    for l in range(s1.shape[0]):
        for copy in copies(l):
            copy.start()

    def level(left, right, l):
        for copy in copies(l):
            copy.wait()
        sweeps(l, (left.at[l], tracers.at[l], right.at[l]), 0, WIDE, wx, wy, middle, third.at[l])

    @pl.when(flag[0] == 1)
    def _():
        pl.loop(0, s1.shape[0])(functools.partial(level, s1, s2))

    @pl.when(flag[0] == 0)
    def _():
        pl.loop(0, s1.shape[0])(functools.partial(level, s2, s1))


def late_kernel(flag, tracers, h1, h2, wx, wy, fields, early, out, s1, middle, third, sems):
    done, count, block = early.shape[0], early.shape[2], 32
    late = s1.shape[0]

    def copy(l):
        return pltpu.make_async_copy(h1.at[l], s1.at[l], sems.at[l])

    for l in range(late):
        copy(l).start()

    def ready_side(left, right, first, last, l):
        sweeps(done + l, (left.at[l], tracers.at[done + l], right.at[l]), first, last, wx, wy, middle.at[l], None)

    def other_side(left, right, first, last, l):
        copy(l).wait()
        sweeps(done + l, (left.at[l], tracers.at[done + l], right.at[l]), first, last, wx, wy, middle.at[l], third.at[l])

    @pl.when(flag[0] == 1)
    def _():
        pl.loop(0, late)(functools.partial(ready_side, s1, h2, CX, WIDE))
        pl.loop(0, late)(functools.partial(other_side, s1, h2, 0, CX))

    @pl.when(flag[0] == 0)
    def _():
        pl.loop(0, late)(functools.partial(ready_side, h2, s1, 0, CX))
        pl.loop(0, late)(functools.partial(other_side, h2, s1, CX, WIDE))

    for x in range(CX):
        for t in range(0, count, block):
            ts = pl.ds(t, block)
            levels = [early[m, x, ts, :] if m < done else third[m - done, x, ts, :] for m in range(LEV)]
            for l in range(LEV):
                value = None
                for m in range(LEV):
                    part = fields[pl.ds((4 + l) * ROWS + m * CX + x, 1), :] * levels[m]
                    value = part if value is None else value + part
                out[l, x, ts, :] = value


def scale_kernel(received, diffused, out, scaled, sems):
    count = diffused.shape[2]
    total = jnp.sum(received[...], axis=0, keepdims=True)
    ratio = total / pltpu.roll(jnp.broadcast_to(total, (8, NY)), NY // 2, 1)[:1]
    lane = lax.broadcasted_iota(jnp.int32, (count, NY), 1)
    row = lax.broadcasted_iota(jnp.int32, (count, NY), 0)
    scale = jnp.sum(jnp.where(lane == row, jnp.broadcast_to(ratio, (count, NY)), 0.0), axis=1, keepdims=True)
    factor = jnp.broadcast_to(scale, (count, NY))
    moves = [pltpu.make_async_copy(scaled.at[l], out.at[l], sems.at[l]) for l in range(LEV)]
    for l in range(LEV):
        for x in range(CX):
            scaled[l, x] = diffused[l, x] * factor
        moves[l].start()
    for move in moves:
        move.wait()


SMEM = pl.BlockSpec(memory_space=pltpu.SMEM)
VMEM = pl.BlockSpec(memory_space=pltpu.VMEM)
ANY = pl.BlockSpec(memory_space=pl.ANY)
HBM = pl.BlockSpec(memory_space=pltpu.HBM)


def work(flops):
    return pl.CostEstimate(flops=flops, bytes_accessed=0, transcendentals=0)


def call(kernel, ins, outs, places=None, scratch=(), limit=VMEM_LIMIT, aliases=(), cost=None):
    places = places or [VMEM] * len(outs)
    return pl.pallas_call(
        kernel,
        out_shape=[s if not isinstance(s, tuple) else pltpu.VMEM(s, F32) if p is VMEM else jax.ShapeDtypeStruct(s, F32) for s, p in zip(outs, places)],
        in_specs=ins,
        out_specs=places,
        scratch_shapes=list(scratch),
        compiler_params=pltpu.CompilerParams(vmem_limit_bytes=limit),
        input_output_aliases=dict(aliases),
        cost_estimate=cost,
    )


def in_hbm(value):
    return pltpu.with_memory_space_constraint(value, pltpu.HBM)


def in_vmem(value):
    return pltpu.with_memory_space_constraint(value, pltpu.VMEM)


def swap(value, axis, partner):
    n = lax.axis_size(axis)
    return lax.ppermute(value, axis, [(i, partner(i, n)) for i in range(n)])


def even_pairs(i, n):
    return i ^ 1


def odd_pairs(i, n):
    return (i + 1) % n if i % 2 else (i - 1) % n


def per_device(tracers, hour_fields, reader_table):
    cells, mine = lax.axis_index("cells"), lax.axis_index("tracers")
    n = lax.axis_size("cells")
    odd = (cells & 1).astype(jnp.int32)[None]
    state = jnp.transpose(tracers, (1, 2, 0, 3))
    count = state.shape[2]
    raw = hour_fields.reshape(NF * ROWS, NY)

    a_levels, c_levels = CHUNKS
    early, late = a_levels + c_levels, LEV - a_levels - c_levels
    flat = state.reshape(LEV, CX * count, NY)

    def other_core(value):
        return swap(value, "tracers", lambda i, n: i ^ 1)

    far = swap(raw, "tracers", lambda i, n: i ^ 2)
    near = other_core(raw)
    def other_core(value):
        return swap(value, "tracers", lambda i, n: i ^ 1)

    far = swap(raw, "tracers", lambda i, n: i ^ 2)
    near = other_core(raw)
    def split(start, levels, *after):
        kernel = functools.partial(split_kernel, start)
        shape = (levels, CX * count, NY)
        return call(kernel, [ANY] * (1 + len(after)), [shape], [ANY], [pltpu.SemaphoreType.DMA((levels,))])(in_hbm(flat), *after)[0]

    chunk = call(
        functools.partial(split_kernel, 0),
        [ANY],
        [(a_levels, CX * count, NY)],
        [ANY],
        [pltpu.SemaphoreType.DMA((a_levels,))],
    )(in_hbm(flat))[0]
    a1 = swap(chunk, "cells", even_pairs)
    a2 = swap(chunk, "cells", odd_pairs)
    rest, mask = call(
        functools.partial(split_mask_kernel, early),
        [SMEM, SMEM, ANY],
        [(late, CX * count, NY), jax.ShapeDtypeStruct((16, NY), jnp.int32)],
        [ANY, VMEM],
        [pltpu.SemaphoreType.DMA((late,))],
    )(reader_table, mine.astype(jnp.int32)[None], in_hbm(flat))
    far = call(gate_kernel, [ANY, ANY], [far.shape], [ANY], aliases={0: 0})(far, rest)[0]
    across = other_core(far)
    fields, message = call(merge_kernel, [VMEM] * 5, [(NF * ROWS, NY), (3 * ROWS, NY)], cost=work(MERGE_FLOPS))(
        mask, raw, near, far, across
    )
    c1 = swap(message, "cells", even_pairs)
    c2 = swap(message, "cells", odd_pairs)
    rest = call(gate_kernel, [ANY, ANY], [rest.shape], [ANY], aliases={0: 0})(rest, message)[0]
    b1 = swap(rest, "cells", even_pairs)
    b2 = swap(rest, "cells", odd_pairs)

    token = call(token_kernel, [ANY, ANY], [(8, NY)])(in_hbm(a1), in_hbm(a2))[0]
    wx, wy, masses = call(
        weights_kernel,
        [SMEM, VMEM, VMEM, VMEM, VMEM, VMEM, ANY],
        [pltpu.HBM((LEV * WIDE * 8, NY), F32), pltpu.HBM((LEV * WIDE * 8, NY), F32), (n, 2 * count)],
    )(odd, message, c1, c2, fields, state, token)
    received = lax.all_to_all(masses, "cells", 0, 0, tiled=True)
    third = call(
        early_kernel,
        [SMEM, VMEM, ANY, ANY, VMEM, VMEM],
        [(early, CX, count, NY)],
        None,
        [
            pltpu.VMEM((early, CX * count, NY), F32),
            pltpu.VMEM((early, CX * count, NY), F32),
            pltpu.VMEM((WIDE, count, NY), F32),
            pltpu.SemaphoreType.DMA((early, 2)),
        ],
        cost=work(KA_FLOPS),
    )(odd, flat, in_hbm(a1), in_hbm(a2), wx, wy)[0]
    diffused = call(
        late_kernel,
        [SMEM, VMEM, ANY] + [VMEM] * 5,
        [(LEV, CX, count, NY)],
        None,
        [
            pltpu.VMEM((late, CX * count, NY), F32),
            pltpu.VMEM((late, WIDE, count, NY), F32),
            pltpu.VMEM((late, CX, count, NY), F32),
            pltpu.SemaphoreType.DMA((late,)),
        ],
        cost=work(KB_FLOPS),
    )(odd, flat, in_hbm(b1), in_vmem(b2), wx, wy, fields, third)[0]
    out = call(
        scale_kernel,
        [VMEM, VMEM],
        [(LEV, CX, count, NY)],
        [HBM],
        [pltpu.VMEM((LEV, CX, count, NY), F32), pltpu.SemaphoreType.DMA((LEV,))],
    )(received, diffused)[0]
    return jnp.transpose(out, (2, 0, 1, 3))


def solution(mesh):
    placed = (
        P("tracers", None, "cells", None),
        P("tracers", None, None, "cells", None),
        P("cells"),
    )
    return jax.shard_map(
        per_device,
        mesh=mesh,
        in_specs=placed,
        out_specs=P("tracers", None, "cells", None),
        check_vma=False,
    )
```

```python
import functools

import jax
import jax.numpy as jnp
from jax import lax
from jax.experimental import pallas as pl
from jax.experimental.pallas import tpu as pltpu
from jax.sharding import PartitionSpec as P

LEV, CX, NY = 6, 6, 128
ROWS = LEV * CX
NF = 10
HALO = 3
WIDE = CX + 2 * HALO
CHUNKS = (2, 0)
KA_FLOPS = 10000000000
KB_FLOPS = 0
MERGE_FLOPS = 0
HEAD = 112
F32 = jnp.float32
VMEM_LIMIT = 10 * 1024 * 1024


def face_weights(c):
    a = jnp.abs(c)
    up = c >= 0
    zero = jnp.zeros_like(c)
    edge = c * (1.0 - a) * (1.0 - a)
    far = -c * a * (1.0 - a)
    mid = c * a * (3.0 - 2.0 * a)
    far_p, far_n = jnp.where(up, far, zero), jnp.where(up, zero, far)
    mid_p, mid_n = jnp.where(up, mid, zero), jnp.where(up, zero, mid)
    s, b = 1.0 / 12.0, 7.0 / 12.0
    return [
        -s * far_p,
        b * far_p - s * edge,
        b * (edge + far_p) - s * far_n + mid_p,
        b * (edge + far_n) - s * far_p + mid_n,
        b * far_n - s * edge,
        -s * far_n,
    ]


def cell_weights(west, east):
    out = []
    for k in range(-3, 4):
        total = None
        if k <= 2:
            total = west[k + 3]
        if k >= -2:
            total = -east[k + 2] if total is None else total - east[k + 2]
        out.append(total + 1.0 if k == 0 else total)
    return out


def wall_weights(c):
    lane = lax.broadcasted_iota(jnp.int32, c.shape, 1)
    last = NY - 1
    c = jnp.where(lane == 0, 0.0, c)
    west = face_weights(c)
    east = [pltpu.roll(a, NY - 1, 1) for a in west]
    b = cell_weights(west, east)
    zero = jnp.zeros_like(c)
    m1, m2, m3 = b[2], b[1], b[0]
    p1, p2, p3 = b[4], b[5], b[6]
    low, high = m2 + m3, p2 + p3
    return [
        jnp.where(lane <= 2, zero, m3),
        jnp.where(lane <= 1, zero, jnp.where(lane == 2, low, m2)),
        jnp.where(lane == 0, zero, jnp.where(lane == 1, m1 + low, m1)),
        b[3] + jnp.where(lane == 0, m1 + low, zero) + jnp.where(lane == last, p1 + high, zero),
        jnp.where(lane == last, zero, jnp.where(lane == last - 1, p1 + high, p1)),
        jnp.where(lane >= last - 1, zero, jnp.where(lane == last - 2, high, p2)),
        jnp.where(lane >= last - 2, zero, p3),
    ]


def split_kernel(start, tracers, part, sems):
    moves = [pltpu.make_async_copy(tracers.at[start + l], part.at[l], sems.at[l]) for l in range(part.shape[0])]
    for move in moves:
        move.start()
    for move in moves:
        move.wait()


def merge_kernel(core_differs, chip_differs, own, near, far, across, fields, message):
    core, chip = core_differs[0] == 0, chip_differs[0] == 0
    here = jnp.where(core, own[...], near[...])
    there = jnp.where(core, far[...], across[...])
    fields[...] = jnp.where(chip, here, there)
    for x in range(CX):
        for f in range(2):
            message[pl.ds(f * ROWS + x * LEV, LEV), :] = fields[pl.ds(f * ROWS + x, LEV, stride=CX), :]
        total = None
        for l in range(LEV):
            thickness = fields[pl.ds(3 * ROWS + l * CX + x, 1), :]
            row = thickness * fields[pl.ds((4 + l) * ROWS + x, LEV, stride=CX), :]
            total = row if total is None else total + row
        message[pl.ds(2 * ROWS + x * LEV, LEV), :] = total


def weights_kernel(flag, own, first, second, fields, tracers, after, wx, wy, masses):
    left_first = flag[0] == 1

    def column(f, x):
        rows = pl.ds(f * ROWS + (x % CX) * LEV, LEV)
        if 0 <= x < CX:
            return own[rows, :]
        a, b = first[rows, :], second[rows, :]
        return jnp.where(left_first, a, b) if x < 0 else jnp.where(left_first, b, a)

    w = {x: column(2, x) for x in range(-6, 12)}
    face = {x: face_weights(0.5 * column(0, x)) for x in range(-5, 12)}
    stride = WIDE * 8

    def adjoint_x(v, lo, hi):
        jump = {f: v[f] - v[f - 1] for f in range(lo - 2, hi + 3)}
        out = {}
        for j in range(lo, hi):
            total = v[j]
            for k in range(-3, 3):
                total = total + face[j - k][k + 3] * jump[j - k]
            out[j] = total
        return out

    v = adjoint_x(w, -HALO, CX + HALO)
    for x in range(-HALO, CX + HALO):
        for k, b in enumerate(cell_weights(face[x], face[x + 1])):
            wx[pl.ds((x + HALO) * 8 + k, LEV, stride=stride), :] = b
        b = wall_weights(column(1, x))
        total = None
        for k in range(7):
            wy[pl.ds((x + HALO) * 8 + k, LEV, stride=stride), :] = b[k]
            part = b[k] * v[x]
            if k != 3:
                part = pltpu.roll(part, (k - 3) % NY, 1)
            total = part if total is None else total + part
        v[x] = total
    v = adjoint_x(v, 0, CX)

    before = after = None
    for l in range(LEV):
        for x in range(CX):
            q = tracers[l, x]
            b = q * fields[pl.ds(2 * ROWS + l * CX + x, 1), :]
            a = q * v[x][l : l + 1, :]
            before = b if before is None else before + b
            after = a if after is None else after + a
    both = jnp.concatenate([before, after], axis=0)
    sums = lax.dot_general(
        jnp.ones((8, NY), F32), both, (((1,), (1,)), ((), ())), precision=lax.Precision.HIGHEST, preferred_element_type=F32
    )
    for i in range(masses.shape[0] // 8):
        masses[pl.ds(8 * i, 8), :] = sums


def stencil(weight, q):
    value = weight(0) * q(0)
    for k in range(1, 7):
        value = value + weight(k) * q(k)
    return value


def sweeps(level, columns, first, last, wx, wy, middle, third):
    count, block = middle.shape[1], 32

    def weights(ref, x):
        return lambda k: ref[pl.ds((level * WIDE + x) * 8 + k, 1), :]

    for t in range(0, count, block):
        ts = pl.ds(t, block)
        for x in range(first, last):
            value = stencil(weights(wx, x), lambda k: columns[(x + k) // CX][pl.ds((x + k) % CX * count + t, block), :])
            middle[x, ts, :] = stencil(weights(wy, x), lambda k: value if k == 3 else pltpu.roll(value, (3 - k) % NY, 1))
        for x in range(CX if third is not None else 0):
            third[x, ts, :] = stencil(weights(wx, x + HALO), lambda k: middle[x + k, ts, :])


def token_kernel(first, second, token):
    token[...] = jnp.zeros_like(token)


def gate_kernel(*refs):
    pass


def early_kernel(flag, tracers, h1, h2, wx, wy, third, s1, s2, middle, sems):
    def copies(l):
        return [pltpu.make_async_copy(h.at[l], s.at[l], sems.at[l, i]) for i, (h, s) in enumerate(((h1, s1), (h2, s2)))]

    for l in range(s1.shape[0]):
        for copy in copies(l):
            copy.start()

    def level(left, right, l):
        for copy in copies(l):
            copy.wait()
        sweeps(l, (left.at[l], tracers.at[l], right.at[l]), 0, WIDE, wx, wy, middle, third.at[l])

    @pl.when(flag[0] == 1)
    def _():
        pl.loop(0, s1.shape[0])(functools.partial(level, s1, s2))

    @pl.when(flag[0] == 0)
    def _():
        pl.loop(0, s1.shape[0])(functools.partial(level, s2, s1))


def late_kernel(done, flag, tracers, h1, h2, wx, wy, third, s1, middle, sems):
    late = s1.shape[0]

    def copy(l):
        return pltpu.make_async_copy(h1.at[l], s1.at[l], sems.at[l])

    for l in range(late):
        copy(l).start()

    def ready_side(left, right, first, last, l):
        sweeps(done + l, (left.at[l], tracers.at[done + l], right.at[l]), first, last, wx, wy, middle.at[l], None)

    def other_side(left, right, first, last, l):
        copy(l).wait()
        sweeps(done + l, (left.at[l], tracers.at[done + l], right.at[l]), first, last, wx, wy, middle.at[l], third.at[l])

    @pl.when(flag[0] == 1)
    def _():
        pl.loop(0, late)(functools.partial(ready_side, s1, h2, CX, WIDE))
        pl.loop(0, late)(functools.partial(other_side, s1, h2, 0, CX))

    @pl.when(flag[0] == 0)
    def _():
        pl.loop(0, late)(functools.partial(ready_side, h2, s1, 0, CX))
        pl.loop(0, late)(functools.partial(other_side, h2, s1, CX, WIDE))


def mix_kernel(received, fields, early, late, out, scaled, sems):
    done, count, block = early.shape[0], early.shape[2], 32
    total = jnp.sum(received[...], axis=0, keepdims=True)
    ratio = total / pltpu.roll(jnp.broadcast_to(total, (8, NY)), NY // 2, 1)[:1]
    lane = lax.broadcasted_iota(jnp.int32, (count, NY), 1)
    row = lax.broadcasted_iota(jnp.int32, (count, NY), 0)
    scale = jnp.sum(jnp.where(lane == row, jnp.broadcast_to(ratio, (count, NY)), 0.0), axis=1, keepdims=True)
    factor = jnp.broadcast_to(scale, (count, NY))
    moves = [pltpu.make_async_copy(scaled.at[x], out.at[:, x], sems.at[x]) for x in range(CX)]
    for x in range(CX):
        for t in range(0, count, block):
            ts = pl.ds(t, block)
            levels = [early[m, x, ts, :] if m < done else late[m - done, x, ts, :] for m in range(LEV)]
            for l in range(LEV):
                value = None
                for m in range(LEV):
                    part = fields[pl.ds((4 + l) * ROWS + m * CX + x, 1), :] * levels[m]
                    value = part if value is None else value + part
                scaled[x, l, ts, :] = value * factor[t : t + block]
        moves[x].start()
    for move in moves:
        move.wait()


SMEM = pl.BlockSpec(memory_space=pltpu.SMEM)
VMEM = pl.BlockSpec(memory_space=pltpu.VMEM)
ANY = pl.BlockSpec(memory_space=pl.ANY)
HBM = pl.BlockSpec(memory_space=pltpu.HBM)


def work(flops):
    return pl.CostEstimate(flops=flops, bytes_accessed=0, transcendentals=0)


def call(kernel, ins, outs, places=None, scratch=(), limit=VMEM_LIMIT, aliases=(), cost=None):
    places = places or [VMEM] * len(outs)
    return pl.pallas_call(
        kernel,
        out_shape=[s if not isinstance(s, tuple) else pltpu.VMEM(s, F32) if p is VMEM else jax.ShapeDtypeStruct(s, F32) for s, p in zip(outs, places)],
        in_specs=ins,
        out_specs=places,
        scratch_shapes=list(scratch),
        compiler_params=pltpu.CompilerParams(vmem_limit_bytes=limit),
        input_output_aliases=dict(aliases),
        cost_estimate=cost,
    )


def in_hbm(value):
    return pltpu.with_memory_space_constraint(value, pltpu.HBM)


def in_vmem(value):
    return pltpu.with_memory_space_constraint(value, pltpu.VMEM)


def swap(value, axis, partner):
    n = lax.axis_size(axis)
    return lax.ppermute(value, axis, [(i, partner(i, n)) for i in range(n)])


def even_pairs(i, n):
    return i ^ 1


def odd_pairs(i, n):
    return (i + 1) % n if i % 2 else (i - 1) % n


def per_device(tracers, hour_fields, reader_table):
    cells, mine = lax.axis_index("cells"), lax.axis_index("tracers")
    n = lax.axis_size("cells")
    odd = (cells & 1).astype(jnp.int32)[None]
    state = jnp.transpose(tracers, (1, 2, 0, 3))
    count = state.shape[2]
    raw = hour_fields.reshape(NF * ROWS, NY)

    a_levels, c_levels = CHUNKS
    early, late = a_levels + c_levels, LEV - a_levels - c_levels
    flat = state.reshape(LEV, CX * count, NY)

    def other_core(value):
        return swap(value, "tracers", lambda i, n: i ^ 1)

    far = swap(raw, "tracers", lambda i, n: i ^ 2)
    near = other_core(raw)
    def other_core(value):
        return swap(value, "tracers", lambda i, n: i ^ 1)

    far = swap(raw, "tracers", lambda i, n: i ^ 2)
    near = other_core(raw)
    def split(start, levels, *after):
        kernel = functools.partial(split_kernel, start)
        shape = (levels, CX * count, NY)
        return call(kernel, [ANY] * (1 + len(after)), [shape], [ANY], [pltpu.SemaphoreType.DMA((levels,))])(in_hbm(flat), *after)[0]

    chunk = call(
        functools.partial(split_kernel, 0),
        [ANY],
        [(a_levels, CX * count, NY)],
        [ANY],
        [pltpu.SemaphoreType.DMA((a_levels,))],
    )(in_hbm(flat))[0]
    a1 = swap(chunk, "cells", even_pairs)
    a2 = swap(chunk, "cells", odd_pairs)
    rest = call(
        functools.partial(split_kernel, early),
        [ANY],
        [(late, CX * count, NY)],
        [ANY],
        [pltpu.SemaphoreType.DMA((late,))],
    )(in_hbm(flat))[0]
    far = call(gate_kernel, [ANY, ANY], [far.shape], [ANY], aliases={0: 0})(far, rest)[0]
    across = other_core(far)
    differ = reader_table ^ mine.astype(jnp.int32)
    core_differs, chip_differs = differ & 1, differ >> 1
    fields, message = call(merge_kernel, [SMEM] * 2 + [VMEM] * 4, [(NF * ROWS, NY), (3 * ROWS, NY)], cost=work(MERGE_FLOPS))(
        core_differs, chip_differs, raw, near, far, across
    )
    c1 = swap(message, "cells", even_pairs)
    c2 = swap(message, "cells", odd_pairs)
    rest = call(gate_kernel, [ANY, ANY], [rest.shape], [ANY], aliases={0: 0})(rest, message)[0]
    b1 = swap(rest, "cells", even_pairs)
    b2 = swap(rest, "cells", odd_pairs)

    token = call(token_kernel, [ANY, ANY], [(8, NY)])(in_hbm(a1), in_hbm(a2))[0]
    wx, wy, masses = call(
        weights_kernel,
        [SMEM, VMEM, VMEM, VMEM, VMEM, VMEM, ANY],
        [pltpu.HBM((LEV * WIDE * 8, NY), F32), pltpu.HBM((LEV * WIDE * 8, NY), F32), (n, 2 * count)],
    )(odd, message, c1, c2, fields, state, token)
    received = lax.all_to_all(masses, "cells", 0, 0, tiled=True)
    third = call(
        early_kernel,
        [SMEM, VMEM, ANY, ANY, VMEM, VMEM],
        [(early, CX, count, NY)],
        None,
        [
            pltpu.VMEM((early, CX * count, NY), F32),
            pltpu.VMEM((early, CX * count, NY), F32),
            pltpu.VMEM((WIDE, count, NY), F32),
            pltpu.SemaphoreType.DMA((early, 2)),
        ],
        cost=work(KA_FLOPS),
    )(odd, flat, in_hbm(a1), in_hbm(a2), wx, wy)[0]
    rest_third = call(
        functools.partial(late_kernel, early),
        [SMEM, VMEM, ANY, VMEM, VMEM, VMEM],
        [(late, CX, count, NY)],
        None,
        [
            pltpu.VMEM((late, CX * count, NY), F32),
            pltpu.VMEM((late, WIDE, count, NY), F32),
            pltpu.SemaphoreType.DMA((late,)),
        ],
        cost=work(KB_FLOPS),
    )(odd, flat, in_hbm(b1), in_vmem(b2), wx, wy)[0]
    out = call(
        mix_kernel,
        [VMEM] * 4,
        [(LEV, CX, count, NY)],
        [HBM],
        [pltpu.VMEM((CX, LEV, count, NY), F32), pltpu.SemaphoreType.DMA((CX,))],
    )(received, fields, third, rest_third)[0]
    return jnp.transpose(out, (2, 0, 1, 3))


def solution(mesh):
    placed = (
        P("tracers", None, "cells", None),
        P("tracers", None, None, "cells", None),
        P("cells"),
    )
    return jax.shard_map(
        per_device,
        mesh=mesh,
        in_specs=placed,
        out_specs=P("tracers", None, "cells", None),
        check_vma=False,
    )
```

```python
import functools

import jax
import jax.numpy as jnp
from jax import lax
from jax.experimental import pallas as pl
from jax.experimental.pallas import tpu as pltpu
from jax.sharding import PartitionSpec as P

LEV, CX, NY = 6, 6, 128
ROWS = LEV * CX
NF = 10
HALO = 3
WIDE = CX + 2 * HALO
EARLY = 2
EARLY_WORK = 10_000_000_000
F32 = jnp.float32
VMEM_LIMIT = 10 * 1024 * 1024


def face_weights(c):
    a = jnp.abs(c)
    up = c >= 0
    zero = jnp.zeros_like(c)
    edge = c * (1.0 - a) * (1.0 - a)
    far = -c * a * (1.0 - a)
    mid = c * a * (3.0 - 2.0 * a)
    far_p, far_n = jnp.where(up, far, zero), jnp.where(up, zero, far)
    mid_p, mid_n = jnp.where(up, mid, zero), jnp.where(up, zero, mid)
    s, b = 1.0 / 12.0, 7.0 / 12.0
    return [
        -s * far_p,
        b * far_p - s * edge,
        b * (edge + far_p) - s * far_n + mid_p,
        b * (edge + far_n) - s * far_p + mid_n,
        b * far_n - s * edge,
        -s * far_n,
    ]


def cell_weights(west, east):
    out = []
    for k in range(-3, 4):
        total = None
        if k <= 2:
            total = west[k + 3]
        if k >= -2:
            total = -east[k + 2] if total is None else total - east[k + 2]
        out.append(total + 1.0 if k == 0 else total)
    return out


def wall_weights(c):
    lane = lax.broadcasted_iota(jnp.int32, c.shape, 1)
    last = NY - 1
    c = jnp.where(lane == 0, 0.0, c)
    west = face_weights(c)
    east = [pltpu.roll(a, NY - 1, 1) for a in west]
    b = cell_weights(west, east)
    zero = jnp.zeros_like(c)
    m1, m2, m3 = b[2], b[1], b[0]
    p1, p2, p3 = b[4], b[5], b[6]
    low, high = m2 + m3, p2 + p3
    return [
        jnp.where(lane <= 2, zero, m3),
        jnp.where(lane <= 1, zero, jnp.where(lane == 2, low, m2)),
        jnp.where(lane == 0, zero, jnp.where(lane == 1, m1 + low, m1)),
        b[3] + jnp.where(lane == 0, m1 + low, zero) + jnp.where(lane == last, p1 + high, zero),
        jnp.where(lane == last, zero, jnp.where(lane == last - 1, p1 + high, p1)),
        jnp.where(lane >= last - 1, zero, jnp.where(lane == last - 2, high, p2)),
        jnp.where(lane >= last - 2, zero, p3),
    ]


def split_kernel(start, tracers, part, sems):
    moves = [pltpu.make_async_copy(tracers.at[start + l], part.at[l], sems.at[l]) for l in range(part.shape[0])]
    for move in moves:
        move.start()
    for move in moves:
        move.wait()


def merge_kernel(core_differs, chip_differs, own, near, far, across, fields, message):
    core, chip = core_differs[0] == 0, chip_differs[0] == 0
    here = jnp.where(core, own[...], near[...])
    there = jnp.where(core, far[...], across[...])
    fields[...] = jnp.where(chip, here, there)
    for x in range(CX):
        for f in range(2):
            message[pl.ds(f * ROWS + x * LEV, LEV), :] = fields[pl.ds(f * ROWS + x, LEV, stride=CX), :]
        total = None
        for l in range(LEV):
            thickness = fields[pl.ds(3 * ROWS + l * CX + x, 1), :]
            row = thickness * fields[pl.ds((4 + l) * ROWS + x, LEV, stride=CX), :]
            total = row if total is None else total + row
        message[pl.ds(2 * ROWS + x * LEV, LEV), :] = total


def weights_kernel(flag, own, first, second, fields, tracers, after, wx, wy, masses):
    left_first = flag[0] == 1

    def column(f, x):
        rows = pl.ds(f * ROWS + (x % CX) * LEV, LEV)
        if 0 <= x < CX:
            return own[rows, :]
        a, b = first[rows, :], second[rows, :]
        return jnp.where(left_first, a, b) if x < 0 else jnp.where(left_first, b, a)

    w = {x: column(2, x) for x in range(-6, 12)}
    face = {x: face_weights(0.5 * column(0, x)) for x in range(-5, 12)}
    stride = WIDE * 8

    def adjoint_x(v, lo, hi):
        jump = {f: v[f] - v[f - 1] for f in range(lo - 2, hi + 3)}
        out = {}
        for j in range(lo, hi):
            total = v[j]
            for k in range(-3, 3):
                total = total + face[j - k][k + 3] * jump[j - k]
            out[j] = total
        return out

    v = adjoint_x(w, -HALO, CX + HALO)
    for x in range(-HALO, CX + HALO):
        for k, b in enumerate(cell_weights(face[x], face[x + 1])):
            wx[pl.ds((x + HALO) * 8 + k, LEV, stride=stride), :] = b
        b = wall_weights(column(1, x))
        total = None
        for k in range(7):
            wy[pl.ds((x + HALO) * 8 + k, LEV, stride=stride), :] = b[k]
            part = b[k] * v[x]
            if k != 3:
                part = pltpu.roll(part, (k - 3) % NY, 1)
            total = part if total is None else total + part
        v[x] = total
    v = adjoint_x(v, 0, CX)

    before = after = None
    for l in range(LEV):
        for x in range(CX):
            q = tracers[l, x]
            b = q * fields[pl.ds(2 * ROWS + l * CX + x, 1), :]
            a = q * v[x][l : l + 1, :]
            before = b if before is None else before + b
            after = a if after is None else after + a
    both = jnp.concatenate([before, after], axis=0)
    sums = lax.dot_general(
        jnp.ones((8, NY), F32), both, (((1,), (1,)), ((), ())), precision=lax.Precision.HIGHEST, preferred_element_type=F32
    )
    for i in range(masses.shape[0] // 8):
        masses[pl.ds(8 * i, 8), :] = sums


def stencil(weight, q):
    value = weight(0) * q(0)
    for k in range(1, 7):
        value = value + weight(k) * q(k)
    return value


def sweeps(level, columns, first, last, wx, wy, middle, third):
    count, block = middle.shape[1], 32

    def weights(ref, x):
        return lambda k: ref[pl.ds((level * WIDE + x) * 8 + k, 1), :]

    for t in range(0, count, block):
        ts = pl.ds(t, block)
        for x in range(first, last):
            value = stencil(weights(wx, x), lambda k: columns[(x + k) // CX][pl.ds((x + k) % CX * count + t, block), :])
            middle[x, ts, :] = stencil(weights(wy, x), lambda k: value if k == 3 else pltpu.roll(value, (3 - k) % NY, 1))
        for x in range(CX if third is not None else 0):
            third[x, ts, :] = stencil(weights(wx, x + HALO), lambda k: middle[x + k, ts, :])


def token_kernel(first, second, token):
    token[...] = jnp.zeros_like(token)


def gate_kernel(*refs):
    pass


def early_kernel(flag, tracers, h1, h2, wx, wy, third, s1, s2, middle, sems):
    def copies(l):
        return [pltpu.make_async_copy(h.at[l], s.at[l], sems.at[l, i]) for i, (h, s) in enumerate(((h1, s1), (h2, s2)))]

    for l in range(s1.shape[0]):
        for copy in copies(l):
            copy.start()

    def level(left, right, l):
        for copy in copies(l):
            copy.wait()
        sweeps(l, (left.at[l], tracers.at[l], right.at[l]), 0, WIDE, wx, wy, middle, third.at[l])

    @pl.when(flag[0] == 1)
    def _():
        pl.loop(0, s1.shape[0])(functools.partial(level, s1, s2))

    @pl.when(flag[0] == 0)
    def _():
        pl.loop(0, s1.shape[0])(functools.partial(level, s2, s1))


def late_kernel(done, flag, tracers, h1, h2, wx, wy, third, s1, middle, sems):
    late = s1.shape[0]

    def copy(l):
        return pltpu.make_async_copy(h1.at[l], s1.at[l], sems.at[l])

    for l in range(late):
        copy(l).start()

    def both_sides(left, right, ready, other):
        def level(l, first, last_sweep):
            columns = (left.at[l], tracers.at[done + l], right.at[l])
            sweeps(done + l, columns, first, first + CX, wx, wy, middle.at[l], last_sweep)

        @pl.loop(0, late)
        def _(l):
            level(l, ready, None)

        @pl.loop(0, late)
        def _(l):
            copy(l).wait()
            level(l, other, third.at[l])

    @pl.when(flag[0] == 1)
    def _():
        both_sides(s1, h2, CX, 0)

    @pl.when(flag[0] == 0)
    def _():
        both_sides(h2, s1, 0, CX)


def mix_kernel(received, fields, early, late, out, scaled, sems):
    done, count, block = early.shape[0], early.shape[2], 32
    total = jnp.sum(received[...], axis=0, keepdims=True)
    ratio = total / pltpu.roll(jnp.broadcast_to(total, (8, NY)), NY // 2, 1)[:1]
    lane = lax.broadcasted_iota(jnp.int32, (count, NY), 1)
    row = lax.broadcasted_iota(jnp.int32, (count, NY), 0)
    scale = jnp.sum(jnp.where(lane == row, jnp.broadcast_to(ratio, (count, NY)), 0.0), axis=1, keepdims=True)
    factor = jnp.broadcast_to(scale, (count, NY))
    moves = [pltpu.make_async_copy(scaled.at[x], out.at[:, x], sems.at[x]) for x in range(CX)]
    for x in range(CX):
        for t in range(0, count, block):
            ts = pl.ds(t, block)
            levels = [early[m, x, ts, :] if m < done else late[m - done, x, ts, :] for m in range(LEV)]
            for l in range(LEV):
                value = None
                for m in range(LEV):
                    part = fields[pl.ds((4 + l) * ROWS + m * CX + x, 1), :] * levels[m]
                    value = part if value is None else value + part
                scaled[x, l, ts, :] = value * factor[t : t + block]
        moves[x].start()
    for move in moves:
        move.wait()


SMEM = pl.BlockSpec(memory_space=pltpu.SMEM)
VMEM = pl.BlockSpec(memory_space=pltpu.VMEM)
ANY = pl.BlockSpec(memory_space=pl.ANY)
HBM = pl.BlockSpec(memory_space=pltpu.HBM)


def work(flops):
    return pl.CostEstimate(flops=flops, bytes_accessed=0, transcendentals=0)


def call(kernel, ins, outs, places=None, scratch=(), limit=VMEM_LIMIT, aliases=(), cost=None):
    places = places or [VMEM] * len(outs)
    return pl.pallas_call(
        kernel,
        out_shape=[s if not isinstance(s, tuple) else pltpu.VMEM(s, F32) if p is VMEM else jax.ShapeDtypeStruct(s, F32) for s, p in zip(outs, places)],
        in_specs=ins,
        out_specs=places,
        scratch_shapes=list(scratch),
        compiler_params=pltpu.CompilerParams(vmem_limit_bytes=limit),
        input_output_aliases=dict(aliases),
        cost_estimate=cost,
    )


def in_hbm(value):
    return pltpu.with_memory_space_constraint(value, pltpu.HBM)


def in_vmem(value):
    return pltpu.with_memory_space_constraint(value, pltpu.VMEM)


def swap(value, axis, partner):
    n = lax.axis_size(axis)
    return lax.ppermute(value, axis, [(i, partner(i, n)) for i in range(n)])


def even_pairs(i, n):
    return i ^ 1


def odd_pairs(i, n):
    return (i + 1) % n if i % 2 else (i - 1) % n


def per_device(tracers, hour_fields, reader_table):
    cells, mine = lax.axis_index("cells"), lax.axis_index("tracers")
    n = lax.axis_size("cells")
    odd = (cells & 1).astype(jnp.int32)[None]
    state = jnp.transpose(tracers, (1, 2, 0, 3))
    count = state.shape[2]
    raw = hour_fields.reshape(NF * ROWS, NY)

    early, late = EARLY, LEV - EARLY
    flat = state.reshape(LEV, CX * count, NY)

    def other_core(value):
        return swap(value, "tracers", lambda i, n: i ^ 1)

    far = swap(raw, "tracers", lambda i, n: i ^ 2)
    near = other_core(raw)
    chunk = call(
        functools.partial(split_kernel, 0),
        [ANY],
        [(early, CX * count, NY)],
        [ANY],
        [pltpu.SemaphoreType.DMA((early,))],
    )(in_hbm(flat))[0]
    a1 = swap(chunk, "cells", even_pairs)
    a2 = swap(chunk, "cells", odd_pairs)
    rest = call(
        functools.partial(split_kernel, early),
        [ANY],
        [(late, CX * count, NY)],
        [ANY],
        [pltpu.SemaphoreType.DMA((late,))],
    )(in_hbm(flat))[0]
    far = call(gate_kernel, [ANY, ANY], [far.shape], [ANY], aliases={0: 0})(far, rest)[0]
    across = other_core(far)
    differ = reader_table ^ mine.astype(jnp.int32)
    core_differs, chip_differs = differ & 1, differ >> 1
    fields, message = call(merge_kernel, [SMEM] * 2 + [VMEM] * 4, [(NF * ROWS, NY), (3 * ROWS, NY)])(
        core_differs, chip_differs, raw, near, far, across
    )
    c1 = swap(message, "cells", even_pairs)
    c2 = swap(message, "cells", odd_pairs)
    rest = call(gate_kernel, [ANY, ANY], [rest.shape], [ANY], aliases={0: 0})(rest, message)[0]
    b1 = swap(rest, "cells", even_pairs)
    b2 = swap(rest, "cells", odd_pairs)

    token = call(token_kernel, [ANY, ANY], [(8, NY)])(in_hbm(a1), in_hbm(a2))[0]
    wx, wy, masses = call(
        weights_kernel,
        [SMEM, VMEM, VMEM, VMEM, VMEM, VMEM, ANY],
        [pltpu.HBM((LEV * WIDE * 8, NY), F32), pltpu.HBM((LEV * WIDE * 8, NY), F32), (n, 2 * count)],
    )(odd, message, c1, c2, fields, state, token)
    received = lax.all_to_all(masses, "cells", 0, 0, tiled=True)
    third = call(
        early_kernel,
        [SMEM, VMEM, ANY, ANY, VMEM, VMEM],
        [(early, CX, count, NY)],
        None,
        [
            pltpu.VMEM((early, CX * count, NY), F32),
            pltpu.VMEM((early, CX * count, NY), F32),
            pltpu.VMEM((WIDE, count, NY), F32),
            pltpu.SemaphoreType.DMA((early, 2)),
        ],
        cost=work(EARLY_WORK),
    )(odd, flat, in_hbm(a1), in_hbm(a2), wx, wy)[0]
    rest_third = call(
        functools.partial(late_kernel, early),
        [SMEM, VMEM, ANY, VMEM, VMEM, VMEM],
        [(late, CX, count, NY)],
        None,
        [
            pltpu.VMEM((late, CX * count, NY), F32),
            pltpu.VMEM((late, WIDE, count, NY), F32),
            pltpu.SemaphoreType.DMA((late,)),
        ],
    )(odd, flat, in_hbm(b1), in_vmem(b2), wx, wy)[0]
    out = call(
        mix_kernel,
        [VMEM] * 4,
        [(LEV, CX, count, NY)],
        [HBM],
        [pltpu.VMEM((CX, LEV, count, NY), F32), pltpu.SemaphoreType.DMA((CX,))],
    )(received, fields, third, rest_third)[0]
    return jnp.transpose(out, (2, 0, 1, 3))


def solution(mesh):
    placed = (
        P("tracers", None, "cells", None),
        P("tracers", None, None, "cells", None),
        P("cells"),
    )
    return jax.shard_map(
        per_device,
        mesh=mesh,
        in_specs=placed,
        out_specs=P("tracers", None, "cells", None),
        check_vma=False,
    )
```

```python
import functools

import jax
import jax.numpy as jnp
from jax import lax
from jax.experimental import pallas as pl
from jax.experimental.pallas import tpu as pltpu
from jax.sharding import PartitionSpec as P

LEV, CX, NY = 6, 6, 128
ROWS = LEV * CX
NF = 10
HALO = 3
WIDE = CX + 2 * HALO
EARLY = 2
EARLY_WORK = 10_000_000_000
F32 = jnp.float32
VMEM_LIMIT = 10 * 1024 * 1024


def face_weights(c):
    a = jnp.abs(c)
    up = c >= 0
    zero = jnp.zeros_like(c)
    edge = c * (1.0 - a) * (1.0 - a)
    far = -c * a * (1.0 - a)
    mid = c * a * (3.0 - 2.0 * a)
    far_p, far_n = jnp.where(up, far, zero), jnp.where(up, zero, far)
    mid_p, mid_n = jnp.where(up, mid, zero), jnp.where(up, zero, mid)
    s, b = 1.0 / 12.0, 7.0 / 12.0
    return [
        -s * far_p,
        b * far_p - s * edge,
        b * (edge + far_p) - s * far_n + mid_p,
        b * (edge + far_n) - s * far_p + mid_n,
        b * far_n - s * edge,
        -s * far_n,
    ]


def cell_weights(west, east):
    out = []
    for k in range(-3, 4):
        total = None
        if k <= 2:
            total = west[k + 3]
        if k >= -2:
            total = -east[k + 2] if total is None else total - east[k + 2]
        out.append(total + 1.0 if k == 0 else total)
    return out


def wall_weights(c):
    lane = lax.broadcasted_iota(jnp.int32, c.shape, 1)
    last = NY - 1
    c = jnp.where(lane == 0, 0.0, c)
    west = face_weights(c)
    east = [pltpu.roll(a, NY - 1, 1) for a in west]
    b = cell_weights(west, east)
    zero = jnp.zeros_like(c)
    m1, m2, m3 = b[2], b[1], b[0]
    p1, p2, p3 = b[4], b[5], b[6]
    low, high = m2 + m3, p2 + p3
    return [
        jnp.where(lane <= 2, zero, m3),
        jnp.where(lane <= 1, zero, jnp.where(lane == 2, low, m2)),
        jnp.where(lane == 0, zero, jnp.where(lane == 1, m1 + low, m1)),
        b[3] + jnp.where(lane == 0, m1 + low, zero) + jnp.where(lane == last, p1 + high, zero),
        jnp.where(lane == last, zero, jnp.where(lane == last - 1, p1 + high, p1)),
        jnp.where(lane >= last - 1, zero, jnp.where(lane == last - 2, high, p2)),
        jnp.where(lane >= last - 2, zero, p3),
    ]


def split_kernel(start, tracers, part, sems):
    moves = [pltpu.make_async_copy(tracers.at[start + l], part.at[l], sems.at[l]) for l in range(part.shape[0])]
    for move in moves:
        move.start()
    for move in moves:
        move.wait()


def merge_kernel(core_differs, chip_differs, own, near, far, across, fields, message):
    core, chip = core_differs[0] == 0, chip_differs[0] == 0
    here = jnp.where(core, own[...], near[...])
    there = jnp.where(core, far[...], across[...])
    fields[pl.ds(0, NF * ROWS), :] = jnp.where(chip, here, there)
    message[pl.ds(3 * ROWS - 4, 8), :] = jnp.zeros((8, NY), F32)
    for x in range(CX):
        for f in range(2):
            message[pl.ds(f * ROWS + x * LEV, LEV), :] = fields[pl.ds(f * ROWS + x, LEV, stride=CX), :]
        total = None
        for l in range(LEV):
            thickness = fields[pl.ds(3 * ROWS + l * CX + x, 1), :]
            row = thickness * fields[pl.ds((4 + l) * ROWS + x, LEV, stride=CX), :]
            total = row if total is None else total + row
        message[pl.ds(2 * ROWS + x * LEV, LEV), :] = total


def weights_kernel(flag, own, first, second, fields, tracers, after, wx, wy, masses):
    left_first = flag[0] == 1

    def column(f, x):
        rows = pl.ds(f * ROWS + (x % CX) * LEV, LEV)
        if 0 <= x < CX:
            return own[rows, :]
        a, b = first[rows, :], second[rows, :]
        return jnp.where(left_first, a, b) if x < 0 else jnp.where(left_first, b, a)

    w = {x: column(2, x) for x in range(-6, 12)}
    face = {x: face_weights(0.5 * column(0, x)) for x in range(-5, 12)}
    stride = WIDE * 8

    def adjoint_x(v, lo, hi):
        jump = {f: v[f] - v[f - 1] for f in range(lo - 2, hi + 3)}
        out = {}
        for j in range(lo, hi):
            total = v[j]
            for k in range(-3, 3):
                total = total + face[j - k][k + 3] * jump[j - k]
            out[j] = total
        return out

    v = adjoint_x(w, -HALO, CX + HALO)
    for x in range(-HALO, CX + HALO):
        for k, b in enumerate(cell_weights(face[x], face[x + 1])):
            wx[pl.ds((x + HALO) * 8 + k, LEV, stride=stride), :] = b
        b = wall_weights(column(1, x))
        total = None
        for k in range(7):
            wy[pl.ds((x + HALO) * 8 + k, LEV, stride=stride), :] = b[k]
            part = b[k] * v[x]
            if k != 3:
                part = pltpu.roll(part, (k - 3) % NY, 1)
            total = part if total is None else total + part
        v[x] = total
    v = adjoint_x(v, 0, CX)

    before = after = None
    for l in range(LEV):
        for x in range(CX):
            q = tracers[l, x]
            b = q * fields[pl.ds(2 * ROWS + l * CX + x, 1), :]
            a = q * v[x][l : l + 1, :]
            before = b if before is None else before + b
            after = a if after is None else after + a
    both = jnp.concatenate([before, after], axis=0)
    sums = lax.dot_general(
        jnp.ones((8, NY), F32), both, (((1,), (1,)), ((), ())), precision=lax.Precision.HIGHEST, preferred_element_type=F32
    )
    for i in range(masses.shape[0] // 8):
        masses[pl.ds(8 * i, 8), :] = sums


def stencil(weight, q):
    value = weight(0) * q(0)
    for k in range(1, 7):
        value = value + weight(k) * q(k)
    return value


def sweeps(level, columns, first, last, wx, wy, middle, third):
    count, block = middle.shape[1], 32

    def weights(ref, x):
        return lambda k: ref[pl.ds((level * WIDE + x) * 8 + k, 1), :]

    for t in range(0, count, block):
        ts = pl.ds(t, block)
        for x in range(first, last):
            value = stencil(weights(wx, x), lambda k: columns[(x + k) // CX][pl.ds((x + k) % CX * count + t, block), :])
            middle[x, ts, :] = stencil(weights(wy, x), lambda k: value if k == 3 else pltpu.roll(value, (3 - k) % NY, 1))
        for x in range(CX if third is not None else 0):
            third[x, ts, :] = stencil(weights(wx, x + HALO), lambda k: middle[x + k, ts, :])


def token_kernel(first, second, token):
    token[...] = jnp.zeros_like(token)


def gate_kernel(*refs):
    pass


def early_kernel(flag, tracers, h1, h2, wx, wy, third, s1, s2, middle, sems):
    def copies(l):
        return [pltpu.make_async_copy(h.at[l], s.at[l], sems.at[l, i]) for i, (h, s) in enumerate(((h1, s1), (h2, s2)))]

    for l in range(s1.shape[0]):
        for copy in copies(l):
            copy.start()

    def level(left, right, l):
        for copy in copies(l):
            copy.wait()
        sweeps(l, (left.at[l], tracers.at[l], right.at[l]), 0, WIDE, wx, wy, middle, third.at[l])

    @pl.when(flag[0] == 1)
    def _():
        pl.loop(0, s1.shape[0])(functools.partial(level, s1, s2))

    @pl.when(flag[0] == 0)
    def _():
        pl.loop(0, s1.shape[0])(functools.partial(level, s2, s1))


def late_kernel(done, flag, tracers, h1, h2, wx, wy, third, s1, middle, sems):
    late = s1.shape[0]

    def copy(l):
        return pltpu.make_async_copy(h1.at[l], s1.at[l], sems.at[l])

    for l in range(late):
        copy(l).start()

    def both_sides(left, right, ready, other):
        def level(l, first, last_sweep):
            columns = (left.at[l], tracers.at[done + l], right.at[l])
            sweeps(done + l, columns, first, first + CX, wx, wy, middle.at[l], last_sweep)

        @pl.loop(0, late)
        def _(l):
            level(l, ready, None)

        @pl.loop(0, late)
        def _(l):
            copy(l).wait()
            level(l, other, third.at[l])

    @pl.when(flag[0] == 1)
    def _():
        both_sides(s1, h2, CX, 0)

    @pl.when(flag[0] == 0)
    def _():
        both_sides(h2, s1, 0, CX)


def mix_kernel(received, fields, early, late, out, scaled, sems):
    done, count, block = early.shape[0], early.shape[2], 32
    total = jnp.sum(received[...], axis=0, keepdims=True)
    ratio = total / pltpu.roll(jnp.broadcast_to(total, (8, NY)), NY // 2, 1)[:1]
    lane = lax.broadcasted_iota(jnp.int32, (count, NY), 1)
    row = lax.broadcasted_iota(jnp.int32, (count, NY), 0)
    scale = jnp.sum(jnp.where(lane == row, jnp.broadcast_to(ratio, (count, NY)), 0.0), axis=1, keepdims=True)
    factor = jnp.broadcast_to(scale, (count, NY))
    moves = [pltpu.make_async_copy(scaled.at[x], out.at[:, x], sems.at[x]) for x in range(CX)]
    for x in range(CX):
        for t in range(0, count, block):
            ts = pl.ds(t, block)
            levels = [early[m, x, ts, :] if m < done else late[m - done, x, ts, :] for m in range(LEV)]
            for l in range(LEV):
                value = None
                for m in range(LEV):
                    part = fields[pl.ds((4 + l) * ROWS + m * CX + x, 1), :] * levels[m]
                    value = part if value is None else value + part
                scaled[x, l, ts, :] = value * factor[t : t + block]
        moves[x].start()
    for move in moves:
        move.wait()


SMEM = pl.BlockSpec(memory_space=pltpu.SMEM)
VMEM = pl.BlockSpec(memory_space=pltpu.VMEM)
ANY = pl.BlockSpec(memory_space=pl.ANY)
HBM = pl.BlockSpec(memory_space=pltpu.HBM)


def work(flops):
    return pl.CostEstimate(flops=flops, bytes_accessed=0, transcendentals=0)


def call(kernel, ins, outs, places=None, scratch=(), limit=VMEM_LIMIT, aliases=(), cost=None):
    places = places or [VMEM] * len(outs)
    return pl.pallas_call(
        kernel,
        out_shape=[s if not isinstance(s, tuple) else pltpu.VMEM(s, F32) if p is VMEM else jax.ShapeDtypeStruct(s, F32) for s, p in zip(outs, places)],
        in_specs=ins,
        out_specs=places,
        scratch_shapes=list(scratch),
        compiler_params=pltpu.CompilerParams(vmem_limit_bytes=limit),
        input_output_aliases=dict(aliases),
        cost_estimate=cost,
    )


def in_hbm(value):
    return pltpu.with_memory_space_constraint(value, pltpu.HBM)


def in_vmem(value):
    return pltpu.with_memory_space_constraint(value, pltpu.VMEM)


def swap(value, axis, partner):
    n = lax.axis_size(axis)
    return lax.ppermute(value, axis, [(i, partner(i, n)) for i in range(n)])


def even_pairs(i, n):
    return i ^ 1


def odd_pairs(i, n):
    return (i + 1) % n if i % 2 else (i - 1) % n


def per_device(tracers, hour_fields, reader_table):
    cells, mine = lax.axis_index("cells"), lax.axis_index("tracers")
    n = lax.axis_size("cells")
    odd = (cells & 1).astype(jnp.int32)[None]
    state = jnp.transpose(tracers, (1, 2, 0, 3))
    count = state.shape[2]
    raw = hour_fields.reshape(NF * ROWS, NY)

    early, late = EARLY, LEV - EARLY
    flat = state.reshape(LEV, CX * count, NY)

    def other_core(value):
        return swap(value, "tracers", lambda i, n: i ^ 1)

    far = swap(raw, "tracers", lambda i, n: i ^ 2)
    near = other_core(raw)
    chunk = call(
        functools.partial(split_kernel, 0),
        [ANY],
        [(early, CX * count, NY)],
        [ANY],
        [pltpu.SemaphoreType.DMA((early,))],
    )(in_hbm(flat))[0]
    a1 = swap(chunk, "cells", even_pairs)
    a2 = swap(chunk, "cells", odd_pairs)
    rest = call(
        functools.partial(split_kernel, early),
        [ANY],
        [(late, CX * count, NY)],
        [ANY],
        [pltpu.SemaphoreType.DMA((late,))],
    )(in_hbm(flat))[0]
    far = call(gate_kernel, [ANY, ANY], [far.shape], [ANY], aliases={0: 0})(far, rest)[0]
    across = other_core(far)
    differ = reader_table ^ mine.astype(jnp.int32)
    core_differs, chip_differs = differ & 1, differ >> 1
    fields, message = call(merge_kernel, [SMEM] * 2 + [VMEM] * 4, [(NF * ROWS + 16, NY), (3 * ROWS + 4, NY)])(
        core_differs, chip_differs, raw, near, far, across
    )
    c1 = swap(message, "cells", even_pairs)
    c2 = swap(message, "cells", odd_pairs)
    rest = call(gate_kernel, [ANY, ANY], [rest.shape], [ANY], aliases={0: 0})(rest, message)[0]
    b1 = swap(rest, "cells", even_pairs)
    b2 = swap(rest, "cells", odd_pairs)

    token = call(token_kernel, [ANY, ANY], [(8, NY)])(in_hbm(a1), in_hbm(a2))[0]
    wx, wy, masses = call(
        weights_kernel,
        [SMEM, VMEM, VMEM, VMEM, VMEM, VMEM, ANY],
        [pltpu.HBM((8 * WIDE * 8, NY), F32), pltpu.HBM((8 * WIDE * 8, NY), F32), (n, 2 * count)],
    )(odd, message, c1, c2, fields, state, token)
    received = lax.all_to_all(masses, "cells", 0, 0, tiled=True)
    third = call(
        early_kernel,
        [SMEM, VMEM, ANY, ANY, VMEM, VMEM],
        [(early, CX, count, NY)],
        None,
        [
            pltpu.VMEM((early, CX * count, NY), F32),
            pltpu.VMEM((early, CX * count, NY), F32),
            pltpu.VMEM((WIDE, count, NY), F32),
            pltpu.SemaphoreType.DMA((early, 2)),
        ],
        cost=work(EARLY_WORK),
    )(odd, flat, in_hbm(a1), in_hbm(a2), wx, wy)[0]
    rest_third = call(
        functools.partial(late_kernel, early),
        [SMEM, VMEM, ANY, VMEM, VMEM, VMEM],
        [(late, CX, count, NY)],
        None,
        [
            pltpu.VMEM((late, CX * count, NY), F32),
            pltpu.VMEM((late, WIDE, count, NY), F32),
            pltpu.SemaphoreType.DMA((late,)),
        ],
    )(odd, flat, in_hbm(b1), in_vmem(b2), wx, wy)[0]
    out = call(
        mix_kernel,
        [VMEM] * 4,
        [(LEV, CX, count, NY)],
        [HBM],
        [pltpu.VMEM((CX, LEV, count, NY), F32), pltpu.SemaphoreType.DMA((CX,))],
    )(received, fields, third, rest_third)[0]
    return jnp.transpose(out, (2, 0, 1, 3))


def solution(mesh):
    placed = (
        P("tracers", None, "cells", None),
        P("tracers", None, None, "cells", None),
        P("cells"),
    )
    return jax.shard_map(
        per_device,
        mesh=mesh,
        in_specs=placed,
        out_specs=P("tracers", None, "cells", None),
        check_vma=False,
    )
```
